32 devices in a mesh: seq: 8 (over z, y), row: 2 (over x), col: 2 (over core).
Axes of the slice: x: 2, y: 2, z: 4, core: 2. Of those that a mesh axis runs over, the one named last changes fastest.
Arguments:
- hidden_in: bfloat16 [4096, 1600], P('seq', ('col', 'row')), may hold values from -6 to 6
- grad_out: bfloat16 [4096, 1600], P('seq', ('col', 'row')), may hold values from -6 to 6
- segment_ids: int32 [4096], replicated, may hold values from 0 to 6, as said below
- pre_gain: float32 [1600], P(('col', 'row')), may hold values from 0.5 to 1.5
- qkv_weight: bfloat16 [1600, 2240], P('col', 'row'), may hold values from -0.15625 to 0.15625
- mixer_in_weight: bfloat16 [1600, 6400], P('col', 'row'), may hold values from -0.15625 to 0.15625
- meta_cache: bfloat16 [2, 128, 320], replicated, may hold values from -6 to 6
- conv_weight: float32 [4, 3200], replicated, may hold values from -3 to 3
- conv_bias: float32 [3200], replicated, may hold values from -3 to 3
- select_weight: float32 [3200, 132], replicated, may hold values from -0.109375 to 0.109375
- step_weight: float32 [100, 3200], replicated, may hold values from -0.625 to 0.625
- step_bias: float32 [3200], replicated, may hold values from -7 to -2
- log_rates: float32 [3200, 16], replicated, may hold values from -4 to 1
- skip_gain: float32 [3200], replicated, may hold values from 0.5 to 1.5
- attn_gain: float32 [1600], replicated, may hold values from 0.5 to 1.5
- mixer_gain: float32 [3200], replicated, may hold values from 0.5 to 1.5
- attn_out_weight: bfloat16 [1600, 1600], P('row', 'col'), may hold values from -0.15625 to 0.15625
- mixer_out_weight: bfloat16 [3200, 1600], P('row', 'col'), may hold values from -0.109375 to 0.109375
- post_gain: float32 [1600], P(('col', 'row')), may hold values from 0.5 to 1.5
- gate_weight: bfloat16 [1600, 5504], P('col', 'row'), may hold values from -0.15625 to 0.15625
- up_weight: bfloat16 [1600, 5504], P('col', 'row'), may hold values from -0.15625 to 0.15625
- down_weight: bfloat16 [5504, 1600], P('row', 'col'), may hold values from -0.078125 to 0.078125
Outputs:
- hidden_out: bfloat16 [4096, 1600], P('seq', ('col', 'row'))
- grad_in: float32 [4096, 1600], P('seq', ('col', 'row'))
- grad_pre_gain: float32 [1600], replicated
- grad_qkv: float32 [1600, 2240], P('col', ('row', 'seq'))
- grad_mixer_in: float32 [1600, 6400], P('col', ('row', 'seq'))
- grad_meta: float32 [2, 128, 320], replicated
- grad_conv_weight: float32 [4, 3200], replicated
- grad_conv_bias: float32 [3200], replicated
- grad_select: float32 [3200, 132], replicated
- grad_step_weight: float32 [100, 3200], replicated
- grad_step_bias: float32 [3200], replicated
- grad_log_rates: float32 [3200, 16], replicated
- grad_skip: float32 [3200], replicated
- grad_attn_gain: float32 [1600], replicated
- grad_mixer_gain: float32 [3200], replicated
- grad_attn_out: float32 [1600, 1600], P('row', ('col', 'seq'))
- grad_mixer_out: float32 [3200, 1600], P('row', ('col', 'seq'))
- grad_post_gain: float32 [1600], replicated
- grad_gate: float32 [1600, 5504], P('col', ('row', 'seq'))
- grad_up: float32 [1600, 5504], P('col', ('row', 'seq'))
- grad_down: float32 [5504, 1600], P('row', ('col', 'seq'))
The draws below stay inside these ranges and needn't reach their ends.
Inputs may be any that keep to these rules, and one draw needn't show every extreme that they name: `segment_ids`: segment numbers start at 0 and never fall along the tokens; the tokens with one number form one document, and documents run across the shards of devices. Some numbers in the range may be unused.
All inputs are finite; a program needn't handle non-finite values.
Results may differ from the reference program's by a relative error of at most 0.014.
Values may be sent and summed in bfloat16 or wider, within the bound.
No kernel may reach another device: no remote copies, remote signals or barrier semaphores. Data moves between devices by JAX's collectives and lax.ppermute only.
A program may use at most 320 MiB of HBM per device.

```python
import jax
import jax.numpy as jnp
from jax import lax

D = 1600
H = 25
KVH = 5
HD = 64
DI = 3200
STATE = 16
DT_RANK = 100
CONV = 4
FF = 5504
META = 128
WIN = 1024
SEQ_LEN = 2048
DOC_MIN = 200
TOKENS = 4096
QKV = 2240


def draw_segment_ids(key, part):
    blocks = TOKENS // SEQ_LEN + 1
    half_len = SEQ_LEN // 2
    key_three, key_two, key_first, key_second = jax.random.split(key, 4)
    three_docs = jax.random.randint(key_three, (blocks, 1), 0, 2)
    cut_two = jax.random.randint(key_two, (blocks, 1), DOC_MIN, half_len - DOC_MIN + 1)
    cut_first = jax.random.randint(key_first, (blocks, 1), DOC_MIN, half_len - 2 * DOC_MIN + 1)
    cut_second = jax.random.randint(key_second, (blocks, 1), cut_first + DOC_MIN, half_len - DOC_MIN + 1)
    position = jnp.arange(SEQ_LEN, dtype=jnp.int32)[None, :]
    local_two = 2 * (position >= cut_two).astype(jnp.int32)
    local_three = (position >= cut_first).astype(jnp.int32) + (position >= cut_second).astype(jnp.int32)
    local_ids = jnp.where(three_docs == 1, local_three, local_two)
    stream = (3 * jnp.arange(blocks, dtype=jnp.int32)[:, None] + local_ids).reshape(blocks * SEQ_LEN)
    offset = 3 * SEQ_LEN // 4
    window = stream[offset:offset + TOKENS]
    return (window - window[0]).astype(jnp.int32)


def level_of(own_key, dims, pieces, least, largest):
    gain = 1.0
    for dim, parts in pieces:
        steps = jax.random.uniform(jax.random.fold_in(jax.random.fold_in(own_key, 6), dim), (parts,), jnp.float32, least / len(pieces), largest / len(pieces))
        gain = gain * jnp.repeat(jnp.exp(steps), dims[dim] // parts).reshape((-1,) + (1,) * (len(dims) - 1 - dim))
    return gain


def centred(rng, shape, scale, reach, pieces=(), kind=jnp.bfloat16):
    factor_of = level_of(rng, shape, pieces, -0.22, 0.18) if pieces else 1.0
    entries = jax.random.normal(rng, shape, jnp.float32) * scale * factor_of
    return jnp.minimum(jnp.maximum(entries, -reach), reach).astype(kind)


def setup_inputs(seed: int = 0) -> dict:
    key_of = jax.random.split(jax.random.key(seed), 23)
    return {
        "hidden_in": centred(key_of[0], (TOKENS, D), 1.0, 6.0, ((0, 8), (1, 4))),
        "grad_out": centred(key_of[1], (TOKENS, D), 1.0, 6.0, ((0, 8), (1, 4))),
        "segment_ids": draw_segment_ids(jax.random.fold_in(key_of[22], 71), 0),
        "pre_gain": jnp.clip(1.0 + 0.1 * jax.random.normal(key_of[3], (D,), jnp.float32), 0.5, 1.5),
        "qkv_weight": centred(key_of[4], (D, QKV), D ** -0.5, 0.15625, ((0, 2), (1, 2))),
        "mixer_in_weight": centred(key_of[5], (D, 2 * DI), D ** -0.5, 0.15625, ((0, 2), (1, 2))),
        "meta_cache": centred(key_of[6], (2, META, KVH * HD), 1.0, 6.0),
        "conv_weight": centred(key_of[7], (CONV, DI), CONV ** -0.5, 3.0, (), jnp.float32),
        "conv_bias": centred(key_of[8], (DI,), 0.5, 3.0, (), jnp.float32),
        "select_weight": centred(key_of[9], (DI, DT_RANK + 2 * STATE), DI ** -0.5, 0.109375, (), jnp.float32),
        "step_weight": centred(key_of[10], (DT_RANK, DI), DT_RANK ** -0.5, 0.625, (), jnp.float32),
        "step_bias": jnp.clip(jax.random.uniform(key_of[11], (DI,), jnp.float32, -7.0, -2.0), -7.0, -2.0),
        "log_rates": jnp.clip(jax.random.uniform(key_of[12], (DI, STATE), jnp.float32, -4.0, 1.0), -4.0, 1.0),
        "skip_gain": jnp.clip(jax.random.uniform(key_of[13], (DI,), jnp.float32, 0.5, 1.5), 0.5, 1.5),
        "attn_gain": jnp.clip(1.0 + 0.1 * jax.random.normal(key_of[14], (D,), jnp.float32), 0.5, 1.5),
        "mixer_gain": jnp.clip(1.0 + 0.1 * jax.random.normal(key_of[15], (DI,), jnp.float32), 0.5, 1.5),
        "attn_out_weight": centred(key_of[16], (D, D), D ** -0.5, 0.15625, ((0, 2), (1, 2))),
        "mixer_out_weight": centred(key_of[17], (DI, D), DI ** -0.5, 0.109375, ((0, 2), (1, 2))),
        "post_gain": jnp.clip(1.0 + 0.1 * jax.random.normal(key_of[18], (D,), jnp.float32), 0.5, 1.5),
        "gate_weight": centred(key_of[19], (D, FF), D ** -0.5, 0.15625, ((0, 2), (1, 2))),
        "up_weight": centred(key_of[20], (D, FF), D ** -0.5, 0.15625, ((0, 2), (1, 2))),
        "down_weight": centred(key_of[21], (FF, D), FF ** -0.5, 0.078125, ((0, 2), (1, 2))),
    }


EPS = 1e-05
NEG = -1e+30
THETA = 10000.0
HIGH = lax.Precision.HIGHEST

@jax.custom_vjp
def low(v):
    return lax.optimization_barrier(v.astype(jnp.bfloat16)).astype(jnp.float32)

@jax.custom_vjp
def low_back(v):
    return v

def low_keep(v):
    return (low(v), None)

def low_pass(kept, grad):
    return (grad,)

def back_keep(v):
    return (v, None)

def back_low(kept, grad):
    return (low(grad),)
low.defvjp(low_keep, low_pass)
low_back.defvjp(back_keep, back_low)

def exact_dot(left_op, right_op):
    return jnp.dot(left_op, right_op, precision=HIGH, preferred_element_type=jnp.float32)

def rms_norm(values, gain_vec):
    return values * lax.rsqrt(lax.optimization_barrier(jnp.mean(values * values, axis=-1, keepdims=True)) + EPS) * gain_vec

def doc_positions(seg_all):
    total = seg_all.shape[0]
    index_all = jnp.arange(total, dtype=jnp.int32)
    starts = jnp.concatenate([jnp.ones((1,), jnp.bool_), seg_all[1:] != seg_all[:-1]])
    start_at = lax.cummax(jnp.where(starts, index_all, jnp.zeros_like(index_all)), axis=0)
    return (index_all - start_at).astype(jnp.int32)

def rope_tables(positions):
    half_width = HD // 2
    frequency = THETA ** (-2.0 * jnp.arange(half_width, dtype=jnp.float32) / HD)
    angles = positions.astype(jnp.float32)[:, None] * frequency[None, :]
    cosine = jnp.concatenate([jnp.cos(angles), jnp.cos(angles)], axis=1)
    sine_tab = jnp.concatenate([jnp.sin(angles), jnp.sin(angles)], axis=1)
    return (cosine, sine_tab)

def rotate_half(values):
    half_width = values.shape[-1] // 2
    return jnp.concatenate([-values[..., half_width:], values[..., :half_width]], axis=-1)

def apply_rope(values, cosine, sine_tab):
    return values * cosine[:, None, :] + rotate_half(values) * sine_tab[:, None, :]

def pair_combine(earlier, latter):
    return (earlier[0] * latter[0], earlier[1] * latter[0] + latter[1])

def linear_run(decay_blk, inject, initial):
    run_prod, run_total = lax.associative_scan(pair_combine, (decay_blk, inject), axis=0)
    return run_total + run_prod * initial[None]

def attention_stream(qkv_seq, seg_seq, positions, meta_cache, attn_gain):
    length = qkv_seq.shape[0]
    kv_width = KVH * HD
    repeats = H // KVH
    cosine, sine_tab = rope_tables(positions)
    queries = low(apply_rope(qkv_seq[:, :D].reshape(length, H, HD), cosine, sine_tab))
    key_rot = low(apply_rope(qkv_seq[:, D:D + kv_width].reshape(length, KVH, HD), cosine, sine_tab))
    value_own = qkv_seq[:, D + kv_width:].reshape(length, KVH, HD)
    keys_all = jnp.repeat(jnp.concatenate([meta_cache[0].reshape(META, KVH, HD), key_rot], axis=0), repeats, axis=1)
    values_all = jnp.repeat(jnp.concatenate([meta_cache[1].reshape(META, KVH, HD), value_own], axis=0), repeats, axis=1)
    row_count = min(512, length)
    key_index = jnp.arange(length, dtype=jnp.int32)

    def query_block(operands):
        query_blk, first_row = operands
        query_index = first_row + jnp.arange(row_count, dtype=jnp.int32)
        query_segs = lax.dynamic_slice(seg_seq, (first_row.astype(jnp.int32),), (row_count,))
        distance = query_index[:, None] - key_index[None, :]
        visible = (seg_seq[None, :] == query_segs[:, None]) & (distance >= 0) & (distance < WIN)
        visible = jnp.concatenate([jnp.ones((row_count, META), jnp.bool_), visible], axis=1)
        scores = jnp.einsum('qhd,khd->hqk', query_blk, keys_all, precision=HIGH) * HD ** (-0.5)
        scores = low_back(jnp.where(visible[None], scores, NEG))
        softmax_out = jax.nn.softmax(scores, axis=-1)
        output = jnp.einsum('hqk,khd->qhd', low(softmax_out), values_all, precision=HIGH)
        return low_back(output).reshape(row_count, D)
    block_count = length // row_count
    outputs = lax.map(jax.checkpoint(query_block), (queries.reshape(block_count, row_count, H, HD), jnp.arange(block_count, dtype=jnp.int32) * row_count))
    attn = outputs.reshape(length, D)
    return low_back(low(rms_norm(attn, attn_gain)))

def mixer_stream(inner_seq, seg_seq, conv_weight, conv_bias, select_weight, step_weight, step_bias, log_rates, skip_gain, mixer_gain):
    length = inner_seq.shape[0]
    tail_rows = CONV - 1
    inner_in = inner_seq[:, :DI]
    gate_z = inner_seq[:, DI:]
    padded = jnp.concatenate([jnp.zeros((tail_rows, DI), inner_in.dtype), inner_in], axis=0)
    seg_padded = jnp.concatenate([jnp.full((tail_rows,), -1, jnp.int32), seg_seq.astype(jnp.int32)])
    conv_sum = conv_bias[None, :]
    for tap_index in range(CONV):
        tap_mask = (seg_padded[tap_index:tap_index + length] == seg_seq).astype(inner_in.dtype)[:, None]
        conv_sum = conv_sum + conv_weight[tap_index][None, :] * padded[tap_index:tap_index + length] * tap_mask
    mixed_in = jax.nn.silu(conv_sum)
    selected = exact_dot(mixed_in, select_weight)
    step_low = selected[:, :DT_RANK]
    in_gate = selected[:, DT_RANK:DT_RANK + STATE]
    out_gate = selected[:, DT_RANK + STATE:]
    step_sizes = jax.nn.softplus(exact_dot(step_low, step_weight) + step_bias[None, :])
    keep_flag = (seg_padded[tail_rows - 1:tail_rows - 1 + length] == seg_seq).astype(inner_in.dtype)
    decay_rates = jnp.exp(log_rates)
    block_len = 16 if length % 16 == 0 else length
    block_count = length // block_len

    def blocked(array):
        return array.reshape((block_count, block_len) + array.shape[1:])

    def block_step(state_in, slab_in):
        step_blk, input_blk, inject_gate, keep_blk, read_gate = slab_in
        decay_blk = jnp.exp(-step_blk[:, :, None] * decay_rates[None]) * keep_blk[:, None, None]
        inject = (step_blk * input_blk)[:, :, None] * inject_gate[:, None, :]
        states = linear_run(decay_blk, inject, state_in)
        return (states[-1], lax.optimization_barrier(jnp.sum(states * read_gate[:, None, :], axis=2)))
    zero_state = jnp.zeros((DI, STATE), inner_in.dtype)
    _, scan_out = lax.scan(jax.checkpoint(block_step), zero_state, (blocked(step_sizes), blocked(mixed_in), blocked(in_gate), blocked(keep_flag), blocked(out_gate)))
    mixed_out = scan_out.reshape(length, DI) + skip_gain[None, :] * mixed_in
    mixer_value = mixed_out * jax.nn.silu(gate_z)
    return low_back(low(rms_norm(mixer_value, mixer_gain)))

def reference(hidden_in, grad_out, segment_ids, pre_gain, qkv_weight, mixer_in_weight, meta_cache, conv_weight, conv_bias, select_weight, step_weight, step_bias, log_rates, skip_gain, attn_gain, mixer_gain, attn_out_weight, mixer_out_weight, post_gain, gate_weight, up_weight, down_weight):
    seg_all = segment_ids.astype(jnp.int32)
    positions = doc_positions(seg_all)

    def forward(resid_in, pre_gain, qkv_weight, mixer_in_weight, meta_cache, conv_weight, conv_bias, select_weight, step_weight, step_bias, log_rates, skip_gain, attn_gain, mixer_gain, attn_out_weight, mixer_out_weight, post_gain, gate_weight, up_weight, down_weight):
        first_low = low(rms_norm(resid_in, pre_gain))
        qkv_all = low_back(low(exact_dot(first_low, qkv_weight)))
        inner_all = low_back(low(exact_dot(first_low, mixer_in_weight)))
        attn_low = attention_stream(qkv_all, seg_all, positions, meta_cache, attn_gain)
        mixer_low = jax.checkpoint(mixer_stream)(inner_all, seg_all, conv_weight, conv_bias, select_weight, step_weight, step_bias, log_rates, skip_gain, mixer_gain)
        mix_sum = low_back(0.5 * (exact_dot(attn_low, attn_out_weight) + exact_dot(mixer_low, mixer_out_weight)))
        resid_mid = resid_in + mix_sum
        second = low(rms_norm(resid_mid, post_gain))
        gate_act = low_back(exact_dot(second, gate_weight))
        up_act = low_back(exact_dot(second, up_weight))
        act_low = low(jax.nn.silu(gate_act) * up_act)
        return resid_mid + exact_dot(act_low, down_weight)
    primals = (hidden_in, pre_gain, qkv_weight, mixer_in_weight, meta_cache, conv_weight, conv_bias, select_weight, step_weight, step_bias, log_rates, skip_gain, attn_gain, mixer_gain, attn_out_weight, mixer_out_weight, post_gain, gate_weight, up_weight, down_weight)
    primals = tuple((entry.astype(jnp.float32) for entry in primals))
    result, pullback = jax.vjp(forward, *primals)
    gradients = pullback(grad_out.astype(jnp.float32))
    return (result.astype(jnp.bfloat16), gradients[0], gradients[1], gradients[2], gradients[3], gradients[4], gradients[5], gradients[6], gradients[7], gradients[8], gradients[9], gradients[10], gradients[11], gradients[12], gradients[13], gradients[14], gradients[15], gradients[16], gradients[17], gradients[18], gradients[19])
```

```python
import functools
import math

import jax
import jax.numpy as jnp
from jax import lax
from jax.experimental import pallas as pl
from jax.experimental.pallas import tpu as pltpu
from jax.sharding import PartitionSpec as P

D = 1600
H = 25
KVH = 5
HD = 64
DI = 3200
STATE = 16
DT_RANK = 100
CONV = 4
META = 128
WIN = 1024


EPS = 1e-05
NEG = -1e30
THETA = 10000.0
HIGH = lax.Precision.HIGHEST
ALL = ("seq", "row", "col")
GROUP = ("row", "col")
LOG2E = 1.4426950408889634
LN2 = 0.6931471805599453
FAR = 1e30
SUB = 8
LANE = 128
VMEM_ASK = 58 * 2**20


def spread_gates(src_ref, dst_ref, length):

    def one(t, carry):
        rows = src_ref[pl.ds(t, SUB, stride=length), :]
        for n in range(STATE):
            dst_ref[t * STATE + n] = jnp.broadcast_to(rows[:, n : n + 1], (SUB, LANE))
        return carry

    lax.fori_loop(0, length, one, 0)


def chunk_decay(rate_ref, total_row):
    return jnp.exp2(rate_ref[...] * total_row)


def scan_totals(length, step_ref, input_ref, keep_ref, gate_ref, rate_ref, end_ref, part_ref, span_ref, wide):
    @pl.when(pl.program_id(0) == 0)
    def _():
        spread_gates(gate_ref, wide, length)

    rates = [jnp.broadcast_to(rate_ref[n : n + 1, :], (SUB, LANE)) for n in range(STATE)]

    def one(t, carry):
        states, span = carry
        rows = pl.ds(t, SUB, stride=length)
        step = step_ref[rows, :]
        lapse = jnp.where(keep_ref[rows, :] > 0.0, step, FAR)
        push = step * input_ref[rows, :]
        states = tuple(
            jnp.exp2(lapse * rates[n]) * states[n] + push * wide[t * STATE + n] for n in range(STATE)
        )
        return (states, span + lapse)

    zero = jnp.zeros((SUB, LANE), jnp.float32)
    states, span = lax.fori_loop(0, length, one, ((zero,) * STATE, zero), unroll=2)
    for n in range(STATE):
        part_ref[0, n] = states[n]
    span_ref[...] = span
    total = jnp.zeros((STATE, LANE), jnp.float32)
    lapsed = jnp.zeros((1, LANE), jnp.float32)
    for k in range(SUB):
        here = span_ref[k : k + 1, :]
        total = chunk_decay(rate_ref, here) * total + part_ref[0, :, k, :]
        lapsed = lapsed + here
    end_ref[0:STATE, :] = total
    end_ref[STATE:, :] = jnp.broadcast_to(lapsed, (SUB, LANE))


def scan_outputs(
    length, step_ref, input_ref, keep_ref, gate_ref, read_ref, rate_ref, part_ref, span_ref, start_ref,
    out_ref, kept_ref, wide, wide_read,
):
    @pl.when(pl.program_id(0) == 0)
    def _():
        spread_gates(gate_ref, wide, length)
        spread_gates(read_ref, wide_read, length)

    state = start_ref[...]
    for k in range(SUB):
        kept_ref[0, 0:STATE, k, :] = state
        state = chunk_decay(rate_ref, span_ref[k : k + 1, :]) * state + part_ref[0, :, k, :]
    rates = [jnp.broadcast_to(rate_ref[n : n + 1, :], (SUB, LANE)) for n in range(STATE)]

    def one(t, states):
        rows = pl.ds(t, SUB, stride=length)
        step = step_ref[rows, :]
        lapse = jnp.where(keep_ref[rows, :] > 0.0, step, FAR)
        push = step * input_ref[rows, :]
        new = []
        seen = [None, None]
        for n in range(STATE):
            value = jnp.exp2(lapse * rates[n]) * states[n] + push * wide[t * STATE + n]
            kept_ref[0, (t + 1) * STATE + n] = value
            part = value * wide_read[t * STATE + n]
            seen[n % 2] = part if seen[n % 2] is None else seen[n % 2] + part
            new.append(value)
        out_ref[rows, :] = seen[0] + seen[1]
        return tuple(new)

    lax.fori_loop(0, length, one, tuple(kept_ref[0, n] for n in range(STATE)), unroll=2)


def adjoint_totals(length, step_ref, dout_ref, keep_ref, read_ref, rate_ref, span_ref, end_ref, part_ref, wide):
    @pl.when(pl.program_id(0) == 0)
    def _():
        spread_gates(read_ref, wide, length)

    rates = [jnp.broadcast_to(rate_ref[n : n + 1, :], (SUB, LANE)) for n in range(STATE)]

    def one(k, carry):
        t = length - 1 - k
        rows = pl.ds(t, SUB, stride=length)
        lapse = jnp.where(keep_ref[rows, :] > 0.0, step_ref[rows, :], FAR)
        dout = dout_ref[rows, :]
        return tuple(
            jnp.exp2(lapse * rates[n]) * (carry[n] + dout * wide[t * STATE + n]) for n in range(STATE)
        )

    zero = jnp.zeros((SUB, LANE), jnp.float32)
    carry = lax.fori_loop(0, length, one, (zero,) * STATE, unroll=2)
    for n in range(STATE):
        part_ref[0, n] = carry[n]
    total = jnp.zeros((STATE, LANE), jnp.float32)
    for k in reversed(range(SUB)):
        total = chunk_decay(rate_ref, span_ref[k : k + 1, :]) * total + part_ref[0, :, k, :]
    end_ref[...] = total


def adjoint_grads(
    length, step_ref, input_ref, keep_ref, dout_ref, gate_ref, read_ref, rate_ref, part_ref, span_ref, start_ref, kept_ref,
    dprod_ref, dstep_ref, drate_ref, dgate_ref, dread_ref, wide, wide_read, entry,
):
    @pl.when(pl.program_id(0) == 0)
    def _():
        spread_gates(gate_ref, wide, length)
        spread_gates(read_ref, wide_read, length)
        dgate_ref[...] = jnp.zeros_like(dgate_ref)
        dread_ref[...] = jnp.zeros_like(dread_ref)

    state = start_ref[...]
    for k in reversed(range(SUB)):
        entry[:, k, :] = state
        state = chunk_decay(rate_ref, span_ref[k : k + 1, :]) * state + part_ref[0, :, k, :]
    half = STATE // 2
    zero = jnp.zeros((SUB, LANE), jnp.float32)
    for low in (0, half):
        rates = [jnp.broadcast_to(rate_ref[n : n + 1, :], (SUB, LANE)) for n in range(low, low + half)]

        def one(j, carry, low=low, rates=rates):
            incoming, rate_sum = carry
            t = length - 1 - j
            rows = pl.ds(t, SUB, stride=length)
            step = step_ref[rows, :]
            lapse = jnp.where(keep_ref[rows, :] > 0.0, step, FAR)
            push = step * input_ref[rows, :]
            dout = dout_ref[rows, :]
            outgoing, sums = [], []
            dprod, dstep = zero, zero
            for i in range(half):
                at = t * STATE + low + i
                adjoint = incoming[i] + dout * wide_read[at]
                dread_ref[at] = dread_ref[at] + kept_ref[0, at + STATE] * dout
                dgate_ref[at] = dgate_ref[at] + adjoint * push
                dprod = dprod + adjoint * wide[at]
                passed = jnp.exp2(lapse * rates[i]) * adjoint
                pull = passed * kept_ref[0, at]
                dstep = dstep + pull * rates[i]
                sums.append(rate_sum[i] + pull * step)
                outgoing.append(passed)
            if low == 0:
                dprod_ref[rows, :] = dprod
                dstep_ref[rows, :] = dstep
            else:
                dprod_ref[rows, :] = dprod_ref[rows, :] + dprod
                dstep_ref[rows, :] = (dstep_ref[rows, :] + dstep) * LN2
            return (tuple(outgoing), tuple(sums))

        start = (tuple(entry[low + i] for i in range(half)), (zero,) * half)
        _, rate_sum = lax.fori_loop(0, length, one, start)
        for i in range(half):
            drate_ref[low + i : low + i + 1, :] = -jnp.sum(rate_sum[i], axis=0, keepdims=True)


def column(rows):
    return pl.BlockSpec((rows, LANE), lambda i: (0, i))


def shared(shape):
    return pl.BlockSpec(shape, lambda i: (0,) * len(shape))


def tile_of(shape):
    return pl.BlockSpec((1,) + shape, lambda i: (i,) + (0,) * len(shape))


def scan_call(body, total, width, in_specs, outs, scratch, args, work):
    length = total // SUB
    params = pltpu.CompilerParams(dimension_semantics=("arbitrary",), vmem_limit_bytes=VMEM_ASK)
    return pl.pallas_call(
        functools.partial(body, length),
        grid=(width // LANE,),
        in_specs=in_specs,
        out_specs=[spec for spec, _ in outs],
        out_shape=[jax.ShapeDtypeStruct(shape, jnp.float32) for _, shape in outs],
        scratch_shapes=[pltpu.VMEM(shape, jnp.float32) for shape in scratch],
        compiler_params=params,
        cost_estimate=pl.CostEstimate(
            flops=work * total * width * STATE,
            transcendentals=total * width * STATE,
            bytes_accessed=16 * total * width,
        ),
    )(*args)


def run_totals(step, mixed, keep, gate, rates):
    total, width = step.shape
    length, tiles = total // SUB, width // LANE
    return scan_call(
        scan_totals,
        total,
        width,
        [column(total), column(total), shared((total, LANE)), shared((total, STATE)), column(STATE)],
        [
            (column(STATE + SUB), (STATE + SUB, width)),
            (tile_of((STATE, SUB, LANE)), (tiles, STATE, SUB, LANE)),
            (column(SUB), (SUB, width)),
        ],
        [(length * STATE, SUB, LANE)],
        (step, mixed, keep, gate, rates),
        6,
    )


def run_outputs(step, mixed, keep, gate, read, rates, part, span, start):
    total, width = step.shape
    length, tiles = total // SUB, width // LANE
    kept = ((length + 1) * STATE, SUB, LANE)
    return scan_call(
        scan_outputs,
        total,
        width,
        [column(total), column(total), shared((total, LANE)), shared((total, STATE)), shared((total, STATE)), column(STATE), tile_of((STATE, SUB, LANE)), column(SUB), column(STATE)],
        [(column(total), (total, width)), (tile_of(kept), (tiles,) + kept)],
        [(length * STATE, SUB, LANE)] * 2,
        (step, mixed, keep, gate, read, rates, part, span, start),
        9,
    )


def run_adjoint_totals(step, dout, keep, read, rates, span):
    total, width = step.shape
    length, tiles = total // SUB, width // LANE
    return scan_call(
        adjoint_totals,
        total,
        width,
        [column(total), column(total), shared((total, LANE)), shared((total, STATE)), column(STATE), column(SUB)],
        [
            (column(STATE), (STATE, width)),
            (tile_of((STATE, SUB, LANE)), (tiles, STATE, SUB, LANE)),
        ],
        [(length * STATE, SUB, LANE)],
        (step, dout, keep, read, rates, span),
        6,
    )


def run_adjoint_grads(step, mixed, keep, dout, gate, read, rates, part, span, start, kept):
    total, width = step.shape
    length = total // SUB
    wide = (length * STATE, SUB, LANE)
    return scan_call(
        adjoint_grads,
        total,
        width,
        [
            column(total), column(total), shared((total, LANE)), column(total),
            shared((total, STATE)), shared((total, STATE)), column(STATE),
            tile_of((STATE, SUB, LANE)), column(SUB), column(STATE), tile_of(kept.shape[1:]),
        ],
        [
            (column(total), (total, width)),
            (column(total), (total, width)),
            (column(STATE), (STATE, width)),
            (shared(wide), wide),
            (shared(wide), wide),
        ],
        [wide, wide, (STATE, SUB, LANE)],
        (step, mixed, keep, dout, gate, read, rates, part, span, start, kept),
        18,
    )


def dot_plain(left_op, right_op):
    return jnp.dot(left_op, right_op, preferred_element_type=jnp.float32)


def dot_left(left_op, right_op):
    return lax.dot_general(
        left_op, right_op, (((0,), (0,)), ((), ())), preferred_element_type=jnp.float32
    )


def dot_right(left_op, right_op):
    return lax.dot_general(
        left_op, right_op, (((1,), (1,)), ((), ())), preferred_element_type=jnp.float32
    )


def exact_dot(left_op, right_op):
    return jnp.dot(left_op, right_op, precision=HIGH, preferred_element_type=jnp.float32)


def exact_left(left_op, right_op):
    return lax.dot_general(
        left_op,
        right_op,
        (((0,), (0,)), ((), ())),
        precision=HIGH,
        preferred_element_type=jnp.float32,
    )


def exact_right(left_op, right_op):
    return lax.dot_general(
        left_op,
        right_op,
        (((1,), (1,)), ((), ())),
        precision=HIGH,
        preferred_element_type=jnp.float32,
    )


def low(values):
    return values.astype(jnp.bfloat16)


def wide(values):
    return values.astype(jnp.float32)


def swapped(values, axis):
    return lax.ppermute(values, axis, [(0, 1), (1, 0)])


def moved(values, axis, distance):
    count = lax.axis_size(axis)
    route = [(i, i + distance) for i in range(count) if 0 <= i + distance < count]
    return lax.ppermute(values, axis, route)


def joined(mine, other, place, axis):
    first = jnp.where(place == 0, mine, other)
    second = jnp.where(place == 0, other, mine)
    return jnp.concatenate([first, second], axis=axis)


def chosen(pieces, place):
    result = pieces[0]
    for index, piece in enumerate(pieces[1:], 1):
        result = jnp.where(place == index, piece, result)
    return result


def pieces_of(values, count, axis):
    size = values.shape[axis] // count
    return [lax.slice_in_dim(values, i * size, (i + 1) * size, axis=axis) for i in range(count)]


def group_total(values):
    over_cols = values + swapped(values, "col")
    return over_cols + swapped(over_cols, "row")


def seq_reduce(values):
    count, place = lax.axis_size("seq"), lax.axis_index("seq")
    parts = values.reshape((count, values.shape[0] // count) + values.shape[1:])
    if count > 8:
        return lax.psum_scatter(wide(parts), "seq", scatter_dimension=0)
    lines = count // 2
    odd, line = place % 2, place // 2
    pairs = parts.reshape((lines, 2) + parts.shape[1:])
    mine = jnp.where(odd == 0, pairs[:, 0], pairs[:, 1])
    other = jnp.where(odd == 0, pairs[:, 1], pairs[:, 0])
    got = lax.ppermute(other, "seq", [(i, i ^ 1) for i in range(count)])
    both = low(wide(mine) + wide(got))
    total = wide(lax.dynamic_index_in_dim(both, line, 0, keepdims=False))
    for step in range(1, lines):
        away = lax.dynamic_index_in_dim(both, (line + step) % lines, 0, keepdims=False)
        route = [(i, ((i // 2 + step) % lines) * 2 + i % 2) for i in range(count)]
        total = total + wide(lax.ppermute(away, "seq", route))
    return total


def rope_tables(positions):
    half_width = HD // 2
    frequency = THETA ** (-2.0 * jnp.arange(half_width, dtype=jnp.float32) / HD)
    angles = positions.astype(jnp.float32)[:, None] * frequency[None, :]
    cosine = jnp.concatenate([jnp.cos(angles), jnp.cos(angles)], axis=1)
    sine_tab = jnp.concatenate([jnp.sin(angles), jnp.sin(angles)], axis=1)
    return (cosine, sine_tab)


def rotate_half(values):
    half_width = values.shape[-1] // 2
    return jnp.concatenate([-values[..., half_width:], values[..., :half_width]], axis=-1)


def apply_rope(values, cosine, sine_tab):
    return values * cosine[:, None, :] + rotate_half(values) * sine_tab[:, None, :]


def rope_back(incoming, cosine, sine_tab):
    return incoming * cosine[:, None, :] - rotate_half(incoming * sine_tab[:, None, :])


def local_norm(values, gain_vec):
    factor = lax.rsqrt(jnp.mean(values * values, axis=1) + EPS)
    return (factor, values * factor[:, None] * gain_vec[None, :])


def local_norm_back(values, factor, gain_vec, incoming):
    weighted = incoming * gain_vec[None, :]
    inner_sum = jnp.mean(weighted * values, axis=1)
    result = factor[:, None] * weighted - values * (factor**3 * inner_sum)[:, None]
    return (result, jnp.sum(incoming * values * factor[:, None], axis=0))


def padded(values, width):
    return jnp.pad(values, ((0, 0), (0, width - values.shape[1])))


def shared_ends(values):
    count = lax.axis_size("seq")
    return lax.all_to_all(
        jnp.broadcast_to(values[None], (count,) + values.shape), "seq", split_axis=0, concat_axis=0
    )


def entering_state(ends, spans, rates, reverse):
    count, place = lax.axis_size("seq"), lax.axis_index("seq")
    state = jnp.zeros_like(ends[0])
    for k in range(count):
        at = count - 1 - k if reverse else k
        reached = at > place if reverse else at < place
        decay = jnp.exp2(rates * spans[at][None, :])
        state = jnp.where(reached, decay * state + ends[at], state)
    return state


def shards(
    hidden_in,
    grad_out,
    segment_ids,
    pre_gain,
    qkv_weight,
    mixer_in_weight,
    meta_cache,
    conv_weight,
    conv_bias,
    select_weight,
    step_weight,
    step_bias,
    log_rates,
    skip_gain,
    attn_gain,
    mixer_gain,
    attn_out_weight,
    mixer_out_weight,
    post_gain,
    gate_weight,
    up_weight,
    down_weight,
):
    row, col, seq = lax.axis_index("row"), lax.axis_index("col"), lax.axis_index("seq")
    tokens = hidden_in.shape[0]
    quarter = DI // 4
    lanes = -(-quarter // LANE) * LANE
    member = 2 * row + col

    def by_row(first, second):
        return jnp.where(row == 0, first, second)

    def row_joined(values):
        return joined(values, swapped(values, "row"), row, 1)

    def col_joined(values):
        return joined(values, swapped(values, "col"), col, 1)

    hidden_m = row_joined(hidden_in)
    gains_m = row_joined(jnp.stack([pre_gain, post_gain]))
    hidden_o = swapped(hidden_m, "col")
    gains_o = swapped(gains_m, "col")

    mixer_parts = pieces_of(mixer_in_weight, 4, 1)
    keep_w = by_row(chosen(mixer_parts[:2], col), chosen(mixer_parts[2:], col))
    give_w = by_row(chosen(mixer_parts[2:], col), chosen(mixer_parts[:2], col))
    keep_send = by_row(chosen(mixer_parts[:2], 1 - col), chosen(mixer_parts[2:], 1 - col))
    give_send = by_row(chosen(mixer_parts[2:], 1 - col), chosen(mixer_parts[:2], 1 - col))
    give_got = swapped(give_send, "col")
    keep_got = swapped(keep_send, "col")
    qkv_parts = pieces_of(qkv_weight, 2, 1)
    qkv_w = chosen(qkv_parts, col)
    qkv_got = swapped(chosen(qkv_parts, 1 - col), "col")

    def split_cols(weight):
        parts = pieces_of(weight, 2, 1)
        return chosen(parts, col), swapped(chosen(parts, 1 - col), "col")

    def split_rows(weight):
        parts = pieces_of(weight, 2, 0)
        return chosen(parts, col), swapped(chosen(parts, 1 - col), "col")

    hm, ho = wide(hidden_m), wide(hidden_o)
    pre_factor = lax.rsqrt((jnp.sum(hm * hm, axis=1) + jnp.sum(ho * ho, axis=1)) / D + EPS)
    first_m = low(hm * pre_factor[:, None] * gains_m[0][None, :])
    first_o = low(ho * pre_factor[:, None] * gains_o[0][None, :])

    given = low(dot_plain(first_m, give_w) + dot_plain(first_o, give_got))
    taken = swapped(given, "row")
    kept_in = low(dot_plain(first_m, keep_w) + dot_plain(first_o, keep_got))
    qkv_part = low(dot_plain(first_m, qkv_w) + dot_plain(first_o, qkv_got))
    qkv_core = lax.all_to_all(qkv_part, GROUP, split_axis=0, concat_axis=1, tiled=True)
    inner_own = by_row(kept_in, taken)
    gate_z = wide(by_row(taken, kept_in))

    grad_m = row_joined(grad_out)
    grad_o = swapped(grad_m, "col")
    gate_w, gate_got = split_cols(gate_weight)
    up_w, up_got = split_cols(up_weight)
    down_w, down_got = split_rows(down_weight)
    mixer_out_w, mixer_out_got = split_rows(mixer_out_weight)
    attn_out_w, attn_out_got = split_rows(attn_out_weight)

    own_tokens = tokens // 4
    devices_back = (WIN + own_tokens - 2) // own_tokens
    halo_rows = devices_back * own_tokens
    tail_rows = CONV - 1
    repeats = H // KVH
    kv_width = KVH * HD
    score_scale = HD ** (-0.5)
    start_row = seq * tokens + member * own_tokens
    seg_padded = jnp.concatenate([jnp.full((halo_rows,), -1, jnp.int32), segment_ids])
    key_segs = lax.dynamic_slice(seg_padded, (start_row,), (halo_rows + own_tokens,))
    query_segs = key_segs[halo_rows:]
    query_glob = start_row + jnp.arange(own_tokens, dtype=jnp.int32)
    key_glob = start_row - halo_rows + jnp.arange(halo_rows + own_tokens, dtype=jnp.int32)
    doc_start = jnp.sum((segment_ids[None, :] < query_segs[:, None]).astype(jnp.int32), axis=1)
    cosine, sine_tab = rope_tables(query_glob - doc_start)
    query_rot = low(
        apply_rope(wide(qkv_core[:, :D]).reshape(own_tokens, H, HD), cosine, sine_tab)
    )
    key_rot = low(
        apply_rope(
            wide(qkv_core[:, D : D + kv_width]).reshape(own_tokens, KVH, HD), cosine, sine_tab
        )
    ).reshape(own_tokens, kv_width)
    pair_own = jnp.concatenate([key_rot, qkv_core[:, D + kv_width :]], axis=1)
    halo = [moved(pair_own, ALL, offset) for offset in range(devices_back, 0, -1)]
    conv_tail = moved(inner_own[tokens - tail_rows :], "seq", 1)

    def channels(values, axis):
        return chosen(pieces_of(values, 4, axis), member)

    conv_w, conv_b = channels(conv_weight, 1), channels(conv_bias, 0)
    select_w, step_w = channels(select_weight, 0), channels(step_weight, 1)
    step_b, skip_g = channels(step_bias, 0), channels(skip_gain, 0)
    mixer_g = channels(mixer_gain, 0)
    decay_rates = jnp.exp(channels(log_rates, 0).T)
    rates = padded(-LOG2E * decay_rates, lanes)

    group_start = seq * tokens
    conv_segs = lax.dynamic_slice(
        seg_padded, (group_start + halo_rows - tail_rows,), (tokens + tail_rows,)
    )
    own_segs = conv_segs[tail_rows:]
    conv_input = wide(jnp.concatenate([conv_tail, inner_own], axis=0))
    tap_masks = [
        wide(conv_segs[tap : tap + tokens] == own_segs)[:, None] for tap in range(CONV)
    ]
    conv_sum = conv_b[None, :]
    for tap in range(CONV):
        conv_sum = conv_sum + conv_w[tap][None, :] * conv_input[tap : tap + tokens] * tap_masks[tap]
    mixed_in = jax.nn.silu(conv_sum)
    selected = group_total(exact_dot(mixed_in, select_w))
    step_low = selected[:, :DT_RANK]
    in_gate = selected[:, DT_RANK : DT_RANK + STATE]
    out_gate = selected[:, DT_RANK + STATE :]
    step_pre = exact_dot(step_low, step_w) + step_b[None, :]
    step_sizes = jax.nn.softplus(step_pre)
    keep_wide = jnp.broadcast_to(tap_masks[CONV - 2], (tokens, LANE))
    step_pad, mixed_pad = padded(step_sizes, lanes), padded(mixed_in, lanes)
    end, scan_part, scan_span = run_totals(step_pad, mixed_pad, keep_wide, in_gate, rates)
    ends = shared_ends(end)
    spans = ends[:, STATE, :]
    state_in = entering_state(ends[:, :STATE], spans, rates, False)

    keys_all = jnp.concatenate([meta_cache[0]] + [h[:, :kv_width] for h in halo] + [key_rot], axis=0)
    values_all = jnp.concatenate(
        [meta_cache[1]] + [h[:, kv_width:] for h in halo] + [pair_own[:, kv_width:]], axis=0
    )
    key_count = keys_all.shape[0]
    distance = query_glob[:, None] - key_glob[None, :]
    visible = (key_segs[None, :] == query_segs[:, None]) & (distance >= 0) & (distance < WIN)
    visible = jnp.concatenate([jnp.ones((own_tokens, META), jnp.bool_), visible], axis=1)
    query_groups = query_rot.reshape(own_tokens, KVH, repeats, HD).transpose(1, 2, 0, 3)
    key_groups = keys_all.reshape(key_count, KVH, HD).transpose(1, 0, 2)
    value_groups = values_all.reshape(key_count, KVH, HD).transpose(1, 0, 2)

    def group_scores(query_grp, key_grp):
        raw_scores = (
            jnp.einsum("rqd,kd->rqk", query_grp, key_grp, preferred_element_type=jnp.float32)
            * score_scale
        )
        return jnp.where(visible[None], raw_scores, NEG)

    def group_forward(operands):
        query_grp, key_grp, value_grp = operands
        scores = group_scores(query_grp, key_grp)
        highest = jnp.max(scores, axis=-1, keepdims=True)
        exponent = jnp.exp(scores - highest)
        totals = jnp.sum(exponent, axis=-1, keepdims=True)
        softmax_out = exponent / totals
        output = jnp.einsum(
            "rqk,kd->rqd", low(softmax_out), value_grp, preferred_element_type=jnp.float32
        )
        return (output, (highest + jnp.log(totals))[..., 0])

    attn_groups, log_totals = lax.map(group_forward, (query_groups, key_groups, value_groups))
    attn_flat = attn_groups.transpose(2, 0, 1, 3).reshape(own_tokens, D)
    attn_factor, attn_normed = local_norm(attn_flat, attn_gain)
    attn_low = low(attn_normed)
    attn_part = lax.all_to_all(attn_low, GROUP, split_axis=1, concat_axis=0, tiled=True)
    attn_rows = col_joined(attn_part)

    scan_out, kept = run_outputs(
        step_pad, mixed_pad, keep_wide, in_gate, out_gate, rates, scan_part, scan_span, state_in
    )
    mixed_out = scan_out[:, :quarter] + skip_g[None, :] * mixed_in
    z_silu = jax.nn.silu(gate_z)
    mixer_value = mixed_out * z_silu
    mixer_mean = lax.psum(jnp.sum(mixer_value * mixer_value, axis=1), GROUP) / DI
    mixer_factor = lax.rsqrt(mixer_mean + EPS)
    mixer_low = low(mixer_value * mixer_factor[:, None] * mixer_g[None, :])
    mixer_rows = col_joined(mixer_low)

    def row_summed(part):
        part = low(part)
        return wide(part) + wide(swapped(part, "row"))

    mix_m = row_summed(
        0.5 * (dot_plain(attn_rows, attn_out_weight) + dot_plain(mixer_rows, mixer_out_weight))
    )
    mix_o = swapped(mix_m, "col")
    resid_m, resid_o = hm + mix_m, ho + mix_o
    post_factor = lax.rsqrt(
        (jnp.sum(resid_m * resid_m, axis=1) + jnp.sum(resid_o * resid_o, axis=1)) / D + EPS
    )
    second_m = low(resid_m * post_factor[:, None] * gains_m[1][None, :])
    second_o = low(resid_o * post_factor[:, None] * gains_o[1][None, :])
    gate_act = dot_plain(second_m, gate_w) + dot_plain(second_o, gate_got)
    up_act = dot_plain(second_m, up_w) + dot_plain(second_o, up_got)
    dact = dot_right(grad_m, down_w) + dot_right(grad_o, down_got)
    sig_gate = jax.nn.sigmoid(gate_act)
    act_low = low(gate_act * sig_gate * up_act)
    dgate_low = low(dact * up_act * sig_gate * (1.0 + gate_act * (1.0 - sig_gate)))
    dup_low = low(dact * gate_act * sig_gate)
    dgate_rows = col_joined(dgate_low)
    dup_rows = col_joined(dup_low)
    act_rows = col_joined(act_low)
    dsecond_m = row_summed(dot_right(dgate_rows, gate_weight) + dot_right(dup_rows, up_weight))
    dsecond_o = swapped(dsecond_m, "col")
    weighted_m = dsecond_m * gains_m[1][None, :]
    weighted_o = dsecond_o * gains_o[1][None, :]
    inner_sum = (jnp.sum(weighted_m * resid_m, axis=1) + jnp.sum(weighted_o * resid_o, axis=1)) / D
    pull_back = (post_factor**3 * inner_sum)[:, None]
    dmid_m = wide(grad_m) + post_factor[:, None] * weighted_m - resid_m * pull_back
    dmid_o = wide(grad_o) + post_factor[:, None] * weighted_o - resid_o * pull_back
    post_part = jnp.sum(dsecond_m * resid_m * post_factor[:, None], axis=0)
    low_m, low_o = low(dmid_m), low(dmid_o)

    dmixer_low = low(0.5 * (dot_right(low_m, mixer_out_w) + dot_right(low_o, mixer_out_got)))
    dattn_part = low(0.5 * (dot_right(low_m, attn_out_w) + dot_right(low_o, attn_out_got)))
    dattn_core = lax.all_to_all(dattn_part, GROUP, split_axis=0, concat_axis=1, tiled=True)

    grad_down = seq_reduce(low(dot_left(grad_m, act_rows)))
    grad_gate = seq_reduce(low(dot_left(dgate_rows, second_m)))
    grad_up = seq_reduce(low(dot_left(dup_rows, second_m)))
    grad_attn_out = seq_reduce(low(0.5 * dot_left(low_m, attn_rows)))
    grad_mixer_out = seq_reduce(low(0.5 * dot_left(low_m, mixer_rows)))

    dmixer_wide = wide(dmixer_low)
    mixer_weighted = dmixer_wide * mixer_g[None, :]
    mixer_sum = lax.psum(jnp.sum(mixer_weighted * mixer_value, axis=1), GROUP) / DI
    dmixer_value = (
        mixer_factor[:, None] * mixer_weighted
        - mixer_value * (mixer_factor**3 * mixer_sum)[:, None]
    )
    mixer_gain_part = jnp.sum(dmixer_wide * mixer_value * mixer_factor[:, None], axis=0)
    sig_z = jax.nn.sigmoid(gate_z)
    dmixed_out = dmixer_value * z_silu
    dgate_z = dmixer_value * mixed_out * sig_z * (1.0 + gate_z * (1.0 - sig_z))
    skip_part = jnp.sum(dmixed_out * mixed_in, axis=0)
    dout_pad = padded(dmixed_out, lanes)
    back_end, back_part = run_adjoint_totals(
        step_pad, dout_pad, keep_wide, out_gate, rates, scan_span
    )
    adjoint_in = entering_state(shared_ends(back_end), spans, rates, True)

    dattn_flat, attn_gain_part = local_norm_back(attn_flat, attn_factor, attn_gain, wide(dattn_core))
    dattn_groups = low(dattn_flat).reshape(own_tokens, KVH, repeats, HD).transpose(1, 2, 0, 3)

    def group_backward(operands):
        query_grp, key_grp, value_grp, dout_grp, lse_grp = operands
        scores = group_scores(query_grp, key_grp)
        softmax_out = jnp.exp(scores - lse_grp[..., None])
        dprobs = jnp.einsum("rqd,kd->rqk", dout_grp, value_grp, preferred_element_type=jnp.float32)
        delta_row = jnp.sum(softmax_out * dprobs, axis=-1, keepdims=True)
        dscores = low(softmax_out * (dprobs - delta_row))
        dquery = (
            jnp.einsum("rqk,kd->rqd", dscores, key_grp, preferred_element_type=jnp.float32)
            * score_scale
        )
        dkey = (
            jnp.einsum("rqk,rqd->kd", dscores, query_grp, preferred_element_type=jnp.float32)
            * score_scale
        )
        dvalue = jnp.einsum(
            "rqk,rqd->kd", low(softmax_out), dout_grp, preferred_element_type=jnp.float32
        )
        return (dquery, dkey, dvalue)

    dquery_groups, dkey_groups, dvalue_groups = lax.map(
        group_backward, (query_groups, key_groups, value_groups, dattn_groups, log_totals)
    )
    dquery_flat = dquery_groups.transpose(2, 0, 1, 3).reshape(own_tokens, H, HD)
    dkey_all = dkey_groups.transpose(1, 0, 2).reshape(key_count, kv_width)
    dvalue_all = dvalue_groups.transpose(1, 0, 2).reshape(key_count, kv_width)
    dpair_all = jnp.concatenate([dkey_all, dvalue_all], axis=1)
    dpair_own = dpair_all[META + halo_rows :]
    for offset in range(1, devices_back + 1):
        low_row = META + (devices_back - offset) * own_tokens
        piece = low(dpair_all[low_row : low_row + own_tokens])
        dpair_own = dpair_own + wide(moved(piece, ALL, -offset))
    dquery_rot = rope_back(dquery_flat, cosine, sine_tab).reshape(own_tokens, D)
    dkey_rot = rope_back(
        dpair_own[:, :kv_width].reshape(own_tokens, KVH, HD), cosine, sine_tab
    ).reshape(own_tokens, kv_width)
    dqkv_core = low(jnp.concatenate([dquery_rot, dkey_rot, dpair_own[:, kv_width:]], axis=1))
    dqkv_part = lax.all_to_all(dqkv_core, GROUP, split_axis=1, concat_axis=0, tiled=True)
    dqkv_rows = col_joined(dqkv_part)
    grad_qkv = seq_reduce(low(dot_left(dqkv_rows, first_m)))

    dproduct, dstep_decay, drates, dgate_wide, dread_wide = run_adjoint_grads(
        step_pad, mixed_pad, keep_wide, dout_pad, in_gate, out_gate, rates, back_part, scan_span,
        adjoint_in, kept,
    )

    def by_token(values):
        summed = jnp.sum(values, axis=-1).reshape(tokens // SUB, STATE, SUB)
        return summed.transpose(2, 0, 1).reshape(tokens, STATE)

    dproduct = dproduct[:, :quarter]
    dsteps = dstep_decay[:, :quarter] + dproduct * mixed_in
    dstep_pre = dsteps * jax.nn.sigmoid(step_pre)
    step_bias_part = jnp.sum(dstep_pre, axis=0)
    step_weight_part = exact_left(step_low, dstep_pre)
    dselected = group_total(
        jnp.concatenate(
            [exact_right(dstep_pre, step_w), by_token(dgate_wide), by_token(dread_wide)], axis=1
        )
    )
    select_part = exact_left(dselected, mixed_in)
    dmixed_in = (
        dmixed_out * skip_g[None, :]
        + dproduct * step_sizes
        + exact_right(dselected, select_w)
    )
    sig_conv = jax.nn.sigmoid(conv_sum)
    dconv_sum = dmixed_in * sig_conv * (1.0 + conv_sum * (1.0 - sig_conv))
    conv_bias_part = jnp.sum(dconv_sum, axis=0)
    conv_rows = []
    dconv_input = jnp.zeros((tokens + tail_rows, quarter), jnp.float32)
    for tap in range(CONV):
        masked_grad = dconv_sum * tap_masks[tap]
        conv_rows.append(jnp.sum(masked_grad * conv_input[tap : tap + tokens], axis=0))
        dconv_input = dconv_input + jnp.pad(
            masked_grad * conv_w[tap][None, :], ((tap, tail_rows - tap), (0, 0))
        )
    dtail_back = moved(dconv_input[:tail_rows], "seq", -1)
    dinner_own = low(
        dconv_input[tail_rows:] + jnp.pad(dtail_back, ((tokens - tail_rows, 0), (0, 0)))
    )
    dz_own = low(dgate_z)
    got_back = swapped(by_row(dz_own, dinner_own), "row")
    near_m = by_row(dinner_own, got_back)
    far_m = by_row(got_back, dz_own)
    near_o, far_o = swapped(near_m, "col"), swapped(far_m, "col")
    near = [jnp.where(col == 0, near_m, near_o), jnp.where(col == 0, near_o, near_m)]
    far = [jnp.where(col == 0, far_m, far_o), jnp.where(col == 0, far_o, far_m)]
    dinner_rows = jnp.concatenate(near + far, axis=1)
    grad_mixer_in = seq_reduce(low(dot_left(dinner_rows, first_m)))

    params = jnp.concatenate(
        [
            select_part,
            step_weight_part,
            drates[:, :quarter] * decay_rates,
            jnp.stack(conv_rows, axis=0),
            conv_bias_part[None],
            step_bias_part[None],
            skip_part[None],
            mixer_gain_part[None],
        ],
        axis=0,
    )
    params = seq_reduce(low(params))
    params = wide(lax.all_gather(low(params), ALL))
    count = lax.axis_size("seq")
    params = params.reshape((count, 4) + params.shape[1:]).transpose(0, 2, 1, 3).reshape(-1, DI)

    dfirst_part = dot_right(dqkv_rows, qkv_weight) + dot_right(dinner_rows, mixer_in_weight)
    first_sum = lax.psum(jnp.sum(dfirst_part * gains_m[0][None, :] * hm, axis=1), GROUP) / D

    def block(values):
        parts = pieces_of(values, 2, 1)
        return by_row(*parts)

    def row_scattered(part):
        parts = pieces_of(part, 2, 1)
        away = low(by_row(parts[1], parts[0]))
        return by_row(*parts) + wide(swapped(away, "row"))

    dfirst = row_scattered(dfirst_part)
    own_hidden = wide(hidden_in)
    grad_in = (
        block(dmid_m)
        + pre_factor[:, None] * dfirst * pre_gain[None, :]
        - own_hidden * (pre_factor**3 * first_sum)[:, None]
    )
    pre_part = jnp.sum(dfirst * own_hidden * pre_factor[:, None], axis=0)
    hidden_out = low(block(resid_m) + row_scattered(dot_plain(act_rows, down_weight)))

    gain_block = pre_gain.shape[0]
    block_pos = (2 * col + row) * gain_block

    def spread(part):
        return lax.dynamic_update_slice(jnp.zeros((D,), jnp.float32), part, (block_pos,))

    meta_part = jnp.stack([dkey_all[:META], dvalue_all[:META]], axis=0)
    post_own = block(post_part[None])[0]
    meta_grad, attn_gain_grad, post_grad = lax.psum(
        (meta_part, attn_gain_part, spread(post_own)), ALL
    )
    pre_grad = lax.psum(spread(pre_part), ALL)
    ranks = DT_RANK + 2 * STATE
    at_rates = ranks + DT_RANK
    at_conv = at_rates + STATE
    return (
        hidden_out,
        grad_in,
        pre_grad,
        grad_qkv.T,
        grad_mixer_in.T,
        meta_grad,
        params[at_conv : at_conv + CONV],
        params[at_conv + CONV],
        params[:ranks].T,
        params[ranks:at_rates],
        params[at_conv + CONV + 1],
        params[at_rates:at_conv].T,
        params[at_conv + CONV + 2],
        attn_gain_grad,
        params[at_conv + CONV + 3],
        grad_attn_out.T,
        grad_mixer_out.T,
        post_grad,
        grad_gate.T,
        grad_up.T,
        grad_down.T,
    )


def solution(mesh):
    in_specs = (
        P("seq", ("col", "row")),
        P("seq", ("col", "row")),
        P(),
        P(("col", "row")),
        P("col", "row"),
        P("col", "row"),
        P(),
        P(),
        P(),
        P(),
        P(),
        P(),
        P(),
        P(),
        P(),
        P(),
        P("row", "col"),
        P("row", "col"),
        P(("col", "row")),
        P("col", "row"),
        P("col", "row"),
        P("row", "col"),
    )
    out_specs = (
        P("seq", ("col", "row")),
        P("seq", ("col", "row")),
        P(),
        P("col", ("row", "seq")),
        P("col", ("row", "seq")),
        P(),
        P(),
        P(),
        P(),
        P(),
        P(),
        P(),
        P(),
        P(),
        P(),
        P("row", ("col", "seq")),
        P("row", ("col", "seq")),
        P(),
        P("col", ("row", "seq")),
        P("col", ("row", "seq")),
        P("row", ("col", "seq")),
    )
    return jax.shard_map(shards, mesh=mesh, in_specs=in_specs, out_specs=out_specs, check_vma=False)
```

```python
import functools
import math

import jax
import jax.numpy as jnp
from jax import lax
from jax.experimental import pallas as pl
from jax.experimental.layout import Layout, with_layout_constraint
from jax.experimental.pallas import tpu as pltpu
from jax.sharding import PartitionSpec as P

D = 1600
H = 25
KVH = 5
HD = 64
DI = 3200
STATE = 16
DT_RANK = 100
CONV = 4
META = 128
WIN = 1024


EPS = 1e-05
NEG = -1e30
THETA = 10000.0
HIGH = lax.Precision.HIGHEST
ALL = ("seq", "row", "col")
GROUP = ("row", "col")
LOG2E = 1.4426950408889634
LN2 = 0.6931471805599453
FAR = 1e30
SUB = 8
LANE = 128
TAIL = CONV - 1
GATES = 2 * STATE
SELECTED = DT_RANK + GATES
VMEM_ASK = 58 * 2**20
SMALL = pl.CostEstimate(flops=1024, transcendentals=0, bytes_accessed=1024)


def nothing(*after, since=None):
    total = 0.0
    for values in after:
        start = (0,) * values.ndim
        if since is not None:
            start = (since,) + start[1:]
        corner = lax.dynamic_slice(values, start, (1,) * values.ndim)
        total = total + jnp.abs(corner.astype(jnp.float32).reshape(()))
    return jnp.minimum(jnp.float32(total), 0.0).astype(jnp.int32)


def exact(left_op, right_op, left_dim, right_dim):
    return lax.dot_general(
        left_op,
        right_op,
        (((left_dim,), (right_dim,)), ((), ())),
        precision=HIGH,
        preferred_element_type=jnp.float32,
    )


def gate_places():
    shape = (GATES, SELECTED)
    found = lax.broadcasted_iota(jnp.int32, shape, 1) - lax.broadcasted_iota(jnp.int32, shape, 0)
    return (found == DT_RANK).astype(jnp.float32)


def token_row(values):
    return exact(jnp.ones((SUB, LANE), jnp.float32), values, 1, 1)


def upright(ref):
    return ref[...].astype(jnp.float32).T


def spread_gates(source, length, *targets):

    def one(t, carry):
        rows = source[pl.ds(t, SUB, stride=length), :]
        for low, target in targets:
            for n in range(STATE):
                column = rows[:, low + n : low + n + 1]
                target[t * STATE + n] = jnp.broadcast_to(column, (SUB, LANE))
        return carry

    lax.fori_loop(0, length, one, 0)


def chunk_decay(rate_ref, total_row):
    return jnp.exp2(rate_ref[...] * total_row)


def convolved(inner_ref, tail_ref, age_ref, weight_ref, bias_ref, padded):
    total = inner_ref.shape[1]
    padded[0:SUB, :] = tail_ref[...]
    padded[SUB : SUB + total, :] = upright(inner_ref)
    result = jnp.broadcast_to(bias_ref[...], (total, LANE))
    for tap in range(CONV):
        found = padded[SUB - TAIL + tap : SUB - TAIL + tap + total, :]
        if tap < TAIL:
            found = jnp.where(age_ref[...] >= TAIL - tap, found, 0.0)
        result = result + weight_ref[tap : tap + 1, :] * found
    return result


def first_mixer(inner_ref, tail_ref, age_ref, weight_ref, bias_ref, select_ref, mixed_ref, picked_ref, padded):
    conv = convolved(inner_ref, tail_ref, age_ref, weight_ref, bias_ref, padded)
    mixed = conv * jax.nn.sigmoid(conv)
    mixed_ref[...] = mixed
    part = exact(mixed, select_ref[...], 1, 1)

    @pl.when(pl.program_id(0) == 0)
    def _():
        picked_ref[...] = part

    @pl.when(pl.program_id(0) > 0)
    def _():
        picked_ref[...] += part


def lapse_of(age_ref, rows, step):
    return jnp.where(age_ref[rows, :] > 0.0, step, FAR)


def scan_totals(
    picked_ref, mixed_ref, age_ref, weight_ref, bias_ref, rate_ref,
    step_ref, pre_ref, end_ref, part_ref, span_ref, gates, wide,
):
    length = mixed_ref.shape[0] // SUB

    @pl.when(pl.program_id(0) == 0)
    def _():
        gates[...] = exact(picked_ref[...], gate_places(), 1, 1)
        spread_gates(gates, length, (0, wide))

    pre = exact(picked_ref[...], weight_ref[...], 1, 0) + bias_ref[...]
    pre_ref[...] = pre
    step_ref[...] = jnp.maximum(pre, 0.0) + jnp.log1p(jnp.exp(-jnp.abs(pre)))
    rates = [jnp.broadcast_to(rate_ref[n : n + 1, :], (SUB, LANE)) for n in range(STATE)]

    def one(t, carry):
        states, span = carry
        rows = pl.ds(t, SUB, stride=length)
        step = step_ref[rows, :]
        lapse = lapse_of(age_ref, rows, step)
        push = step * mixed_ref[rows, :]
        states = tuple(
            jnp.exp2(lapse * rates[n]) * states[n] + push * wide[t * STATE + n] for n in range(STATE)
        )
        return (states, span + lapse)

    zero = jnp.zeros((SUB, LANE), jnp.float32)
    states, span = lax.fori_loop(0, length, one, ((zero,) * STATE, zero), unroll=2)
    for n in range(STATE):
        part_ref[0, n] = states[n]
    span_ref[...] = span
    total = jnp.zeros((STATE, LANE), jnp.float32)
    lapsed = jnp.zeros((1, LANE), jnp.float32)
    for k in range(SUB):
        here = span_ref[k : k + 1, :]
        total = chunk_decay(rate_ref, here) * total + part_ref[0, :, k, :]
        lapsed = lapsed + here
    end_ref[0:STATE, :] = total
    end_ref[STATE:, :] = jnp.broadcast_to(lapsed, (SUB, LANE))


def scan_outputs(
    step_ref, mixed_ref, age_ref, picked_ref, rate_ref, part_ref, span_ref, start_ref, skip_ref, z_ref,
    mixed_out_ref, value_ref, square_ref, kept_ref, gates, wide, wide_read, squares,
):
    length = mixed_ref.shape[0] // SUB

    @pl.when(pl.program_id(0) == 0)
    def _():
        gates[...] = exact(picked_ref[...], gate_places(), 1, 1)
        spread_gates(gates, length, (0, wide), (STATE, wide_read))
        squares[...] = jnp.zeros_like(squares)

    state = start_ref[...]
    for k in range(SUB):
        kept_ref[0, 0:STATE, k, :] = state
        state = chunk_decay(rate_ref, span_ref[k : k + 1, :]) * state + part_ref[0, :, k, :]
    rates = [jnp.broadcast_to(rate_ref[n : n + 1, :], (SUB, LANE)) for n in range(STATE)]

    def one(t, states):
        rows = pl.ds(t, SUB, stride=length)
        step = step_ref[rows, :]
        lapse = lapse_of(age_ref, rows, step)
        push = step * mixed_ref[rows, :]
        new = []
        seen = [None, None]
        for n in range(STATE):
            value = jnp.exp2(lapse * rates[n]) * states[n] + push * wide[t * STATE + n]
            kept_ref[0, (t + 1) * STATE + n] = value
            part = value * wide_read[t * STATE + n]
            seen[n % 2] = part if seen[n % 2] is None else seen[n % 2] + part
            new.append(value)
        mixed_out_ref[rows, :] = seen[0] + seen[1]
        return tuple(new)

    lax.fori_loop(0, length, one, tuple(kept_ref[0, n] for n in range(STATE)), unroll=2)
    mixed_out = mixed_out_ref[...] + skip_ref[...] * mixed_ref[...]
    mixed_out_ref[...] = mixed_out
    z = upright(z_ref)
    value = mixed_out * z * jax.nn.sigmoid(z)
    value_ref[...] = value
    squares[...] += value * value

    @pl.when(pl.program_id(0) == pl.num_programs(0) - 1)
    def _():
        square_ref[...] = token_row(squares[...])


def normed(value_ref, factor_ref, gain_ref, out_ref):
    out_ref[...] = (value_ref[...].T * factor_ref[0:1, :] * gain_ref[...]).astype(out_ref.dtype)


def norm_pull(value_ref, grad_ref, gain_ref, sum_ref, sums):
    part = upright(grad_ref) * gain_ref[...] * value_ref[...]

    @pl.when(pl.program_id(0) == 0)
    def _():
        sums[...] = part

    @pl.when(pl.program_id(0) > 0)
    def _():
        sums[...] += part

    @pl.when(pl.program_id(0) == pl.num_programs(0) - 1)
    def _():
        sum_ref[...] = token_row(sums[...])


def adjoint_totals(
    value_ref, grad_ref, gain_ref, stats_ref, z_ref, mixed_out_ref, mixed_ref,
    step_ref, age_ref, picked_ref, rate_ref, span_ref,
    dmixed_ref, dz_ref, side_ref, end_ref, part_ref, gates, wide, factors, pulls,
):
    total = mixed_ref.shape[0]
    length = total // SUB

    @pl.when(pl.program_id(0) == 0)
    def _():
        gates[...] = exact(picked_ref[...], gate_places(), 1, 1)
        spread_gates(gates, length, (STATE, wide))
        columns = stats_ref[...].T
        factors[...] = jnp.broadcast_to(columns[:, 0:1], (total, LANE))
        pulls[...] = jnp.broadcast_to(columns[:, 1:2], (total, LANE))

    grad, z, value = upright(grad_ref), upright(z_ref), value_ref[...]
    dvalue = factors[...] * gain_ref[...] * grad - value * pulls[...]
    sig = jax.nn.sigmoid(z)
    dmixed = dvalue * z * sig
    dmixed_ref[...] = dmixed
    dz = dvalue * mixed_out_ref[...] * sig * (1.0 + z * (1.0 - sig))
    dz_ref[...] = dz.T.astype(dz_ref.dtype)
    side_ref[...] = jnp.zeros_like(side_ref)
    side_ref[0:1, :] = jnp.sum(dmixed * mixed_ref[...], axis=0, keepdims=True)
    side_ref[1:2, :] = jnp.sum(grad * value * factors[...], axis=0, keepdims=True)
    rates = [jnp.broadcast_to(rate_ref[n : n + 1, :], (SUB, LANE)) for n in range(STATE)]

    def one(k, carry):
        t = length - 1 - k
        rows = pl.ds(t, SUB, stride=length)
        lapse = lapse_of(age_ref, rows, step_ref[rows, :])
        dout = dmixed_ref[rows, :]
        return tuple(
            jnp.exp2(lapse * rates[n]) * (carry[n] + dout * wide[t * STATE + n]) for n in range(STATE)
        )

    zero = jnp.zeros((SUB, LANE), jnp.float32)
    carry = lax.fori_loop(0, length, one, (zero,) * STATE, unroll=2)
    for n in range(STATE):
        part_ref[0, n] = carry[n]
    ends = jnp.zeros((STATE, LANE), jnp.float32)
    for k in reversed(range(SUB)):
        ends = chunk_decay(rate_ref, span_ref[k : k + 1, :]) * ends + part_ref[0, :, k, :]
    end_ref[...] = ends


def adjoint_grads(
    step_ref, mixed_ref, age_ref, dout_ref, picked_ref, rate_ref, part_ref, span_ref, start_ref, kept_ref,
    pre_ref, weight_ref, skip_ref,
    direct_ref, side_ref, drate_ref, dweight_ref, dpicked_ref,
    gates, wide, wide_read, entry, dgate_ref, dread_ref, dprod_ref, dstep_ref,
):
    length = mixed_ref.shape[0] // SUB

    @pl.when(pl.program_id(0) == 0)
    def _():
        gates[...] = exact(picked_ref[...], gate_places(), 1, 1)
        spread_gates(gates, length, (0, wide), (STATE, wide_read))
        dgate_ref[...] = jnp.zeros_like(dgate_ref)
        dread_ref[...] = jnp.zeros_like(dread_ref)

    state = start_ref[...]
    for k in reversed(range(SUB)):
        entry[:, k, :] = state
        state = chunk_decay(rate_ref, span_ref[k : k + 1, :]) * state + part_ref[0, :, k, :]
    half = STATE // 2
    zero = jnp.zeros((SUB, LANE), jnp.float32)
    for low in (0, half):
        rates = [jnp.broadcast_to(rate_ref[n : n + 1, :], (SUB, LANE)) for n in range(low, low + half)]

        def one(j, carry, low=low, rates=rates):
            incoming, rate_sum = carry
            t = length - 1 - j
            rows = pl.ds(t, SUB, stride=length)
            step = step_ref[rows, :]
            lapse = lapse_of(age_ref, rows, step)
            push = step * mixed_ref[rows, :]
            dout = dout_ref[rows, :]
            outgoing, sums = [], []
            dprod, dstep = zero, zero
            for i in range(half):
                at = t * STATE + low + i
                adjoint = incoming[i] + dout * wide_read[at]
                dread_ref[at] = dread_ref[at] + kept_ref[0, at + STATE] * dout
                dgate_ref[at] = dgate_ref[at] + adjoint * push
                dprod = dprod + adjoint * wide[at]
                passed = jnp.exp2(lapse * rates[i]) * adjoint
                pull = passed * kept_ref[0, at]
                dstep = dstep + pull * rates[i]
                sums.append(rate_sum[i] + pull * step)
                outgoing.append(passed)
            if low == 0:
                dprod_ref[rows, :] = dprod
                dstep_ref[rows, :] = dstep
            else:
                dprod_ref[rows, :] = dprod_ref[rows, :] + dprod
                dstep_ref[rows, :] = (dstep_ref[rows, :] + dstep) * LN2
            return (tuple(outgoing), tuple(sums))

        start = (tuple(entry[low + i] for i in range(half)), (zero,) * half)
        _, rate_sum = lax.fori_loop(0, length, one, start)
        for i in range(half):
            found = jnp.sum(rate_sum[i], axis=0, keepdims=True)
            drate_ref[low + i : low + i + 1, :] = found * rate_ref[low + i : low + i + 1, :] * LN2

    dprod = dprod_ref[...]
    direct_ref[...] = dout_ref[...] * skip_ref[...] + dprod * step_ref[...]
    dpre = (dstep_ref[...] + dprod * mixed_ref[...]) * jax.nn.sigmoid(pre_ref[...])
    side_ref[...] = jnp.broadcast_to(jnp.sum(dpre, axis=0, keepdims=True), (SUB, LANE))
    dweight_ref[...] = exact(picked_ref[...], dpre, 0, 0)
    part = exact(dpre, weight_ref[...], 1, 1)

    @pl.when(pl.program_id(0) == 0)
    def _():
        dpicked_ref[...] = part

    @pl.when(pl.program_id(0) > 0)
    def _():
        dpicked_ref[...] += part

    @pl.when(pl.program_id(0) == pl.num_programs(0) - 1)
    def _():
        place = lax.broadcasted_iota(jnp.int32, (SUB, GATES), 1)

        def gather(t, carry):
            found = jnp.zeros((SUB, GATES), jnp.float32)
            for base, source in ((0, dgate_ref), (STATE, dread_ref)):
                for n in range(STATE):
                    summed = jnp.sum(source[t * STATE + n], axis=1, keepdims=True)
                    found = jnp.where(place == base + n, summed, found)
            gates[pl.ds(t, SUB, stride=length), :] = found
            return carry

        lax.fori_loop(0, length, gather, 0)
        dpicked_ref[...] += exact(gates[...], gate_places(), 1, 0)


def last_mixer(
    inner_ref, tail_ref, age_ref, weight_ref, bias_ref, select_ref, dpicked_ref, direct_ref, mixed_ref,
    dinner_ref, edge_ref, side_ref, dselect_ref, padded, spilled,
):
    total = mixed_ref.shape[0]
    conv = convolved(inner_ref, tail_ref, age_ref, weight_ref, bias_ref, padded)
    sig = jax.nn.sigmoid(conv)
    dmixed = direct_ref[...] + exact(dpicked_ref[...], select_ref[...], 1, 0)
    dconv = dmixed * sig * (1.0 + conv * (1.0 - sig))
    dselect_ref[...] = exact(dpicked_ref[...], mixed_ref[...], 0, 0)
    side_ref[...] = jnp.zeros_like(side_ref)
    side_ref[CONV : CONV + 1, :] = jnp.sum(dconv, axis=0, keepdims=True)
    spilled[...] = jnp.zeros_like(spilled)
    for tap in range(CONV):
        at = slice(SUB - TAIL + tap, SUB - TAIL + tap + total)
        masked = dconv
        if tap < TAIL:
            masked = jnp.where(age_ref[...] >= TAIL - tap, dconv, 0.0)
        side_ref[tap : tap + 1, :] = jnp.sum(masked * padded[at, :], axis=0, keepdims=True)
        spilled[at, :] += masked * weight_ref[tap : tap + 1, :]
    edge_ref[0:SUB, :] = spilled[0:SUB, :]
    edge_ref[SUB:, :] = spilled[total : total + SUB, :]
    dinner_ref[...] = spilled[SUB:, :].T.astype(dinner_ref.dtype)


def column(rows):
    return pl.BlockSpec((rows, LANE), lambda i: (0, i))


def banded(rows, width):
    return pl.BlockSpec((rows, width), lambda i: (i, 0))


def shared(shape):
    return pl.BlockSpec(shape, lambda i: (0,) * len(shape))


def tile_of(shape):
    return pl.BlockSpec((1,) + shape, lambda i: (i,) + (0,) * len(shape))


def run_tiles(body, steps, ins, outs, scratch=(), after=()):
    args = [value for value, _ in ins]
    specs = [spec for _, spec in ins]
    args = args + list(after)
    specs = specs + [pl.BlockSpec(memory_space=pl.ANY)] * len(after)

    def kernel(*refs):
        body(*refs[: len(ins)], *refs[len(args) :])

    return pl.pallas_call(
        kernel,
        grid=(steps,),
        in_specs=specs,
        out_specs=[spec for _, _, spec in outs],
        out_shape=[jax.ShapeDtypeStruct(shape, dtype) for shape, dtype, _ in outs],
        scratch_shapes=[pltpu.VMEM(shape, jnp.float32) for shape in scratch],
        compiler_params=pltpu.CompilerParams(
            dimension_semantics=("arbitrary",), vmem_limit_bytes=VMEM_ASK
        ),
        cost_estimate=SMALL,
    )(*args)


def handed_on(source_ref, target_ref):
    target_ref[...] = source_ref[...]


def held_until(values, after):
    whole = shared(values.shape)
    return run_tiles(handed_on, 1, [(values, whole)], [(values.shape, values.dtype, whole)], (), after)[0]


class Mixer:

    def __init__(self, tokens, width, age, inner, tail, z, conv_w, conv_b, select_w, step_w, step_b, rates, skip, gain):
        self.tokens, self.width, self.tiles = tokens, width, width // LANE
        self.long = column(tokens)
        self.tall = banded(LANE, tokens)
        self.row = column(1)
        picked = shared((tokens, SELECTED))
        self.picked_spec = picked
        self.age = (age, shared((tokens, LANE)))
        self.conv = [
            (inner, self.tall), (tail, column(SUB)), self.age, (conv_w, column(CONV)), (conv_b, self.row),
            (select_w, column(SELECTED)),
        ]
        self.z = (z, self.tall)
        self.step_w = (step_w, column(SELECTED))
        self.step_b = (step_b, self.row)
        self.rates = (rates, column(STATE))
        self.skip, self.gain = (skip, self.row), (gain, self.row)
        self.wide = (tokens // SUB * STATE, SUB, LANE)
        self.states = (STATE, SUB, LANE)
        self.buffer = (tokens + SUB, LANE)

    def f32(self, rows, spec=None):
        return ((rows, self.width), jnp.float32, spec or column(rows))

    def low_out(self):
        return ((self.width, self.tokens), jnp.bfloat16, self.tall)

    def row_out(self):
        return ((SUB, self.tokens), jnp.float32, shared((SUB, self.tokens)))

    def picked_out(self):
        return ((self.tokens, SELECTED), jnp.float32, self.picked_spec)

    def states_out(self):
        return ((self.tiles,) + self.states, jnp.float32, tile_of(self.states))

    def run(self, body, ins, outs, scratch=(), after=()):
        return run_tiles(body, self.tiles, ins, outs, scratch, after)

    def first(self):
        mixed, picked = self.run(first_mixer, self.conv, [self.f32(self.tokens), self.picked_out()], [self.buffer])
        self.mixed = (mixed, self.long)
        return mixed, picked

    def totals(self, picked, after):
        self.picked = (picked, self.picked_spec)
        step, pre, end, part, span = self.run(
            scan_totals,
            [self.picked, self.mixed, self.age, self.step_w, self.step_b, self.rates],
            [self.f32(self.tokens)] * 2 + [self.f32(STATE + SUB), self.states_out(), self.f32(SUB)],
            [(self.tokens, GATES), self.wide],
            after,
        )
        self.step, self.pre = (step, self.long), (pre, self.long)
        self.part, self.span = (part, tile_of(self.states)), (span, column(SUB))
        return end

    def outputs(self, state_in, after):
        kept_shape = (self.wide[0] + STATE, SUB, LANE)
        mixed_out, value, squares, kept = self.run(
            scan_outputs,
            [self.step, self.mixed, self.age, self.picked, self.rates, self.part, self.span,
             (state_in, column(STATE)), self.skip, self.z],
            [self.f32(self.tokens)] * 2 + [self.row_out(),
             ((self.tiles,) + kept_shape, jnp.float32, tile_of(kept_shape))],
            [(self.tokens, GATES), self.wide, self.wide, (self.tokens, LANE)],
            after,
        )
        self.mixed_out, self.value = (mixed_out, self.long), (value, self.long)
        self.kept = (kept, tile_of(kept_shape))
        return squares[0]

    def normed(self, factor, gain):
        factor = jnp.broadcast_to(factor[None, :], (SUB, self.tokens))
        return self.run(
            normed,
            [self.value, (factor, shared((SUB, self.tokens))), (gain[:, None], banded(LANE, 1))],
            [self.low_out()],
        )[0]

    def norm_pull(self, grad):
        self.grad = (grad, self.tall)
        return self.run(
            norm_pull, [self.value, self.grad, self.gain], [self.row_out()], [(self.tokens, LANE)]
        )[0][0]

    def back_totals(self, factor, pull, after):
        stats = jnp.concatenate(
            [factor[None], pull[None], jnp.zeros((SUB - 2, self.tokens), jnp.float32)], axis=0
        )
        dmixed, dz, side, end, part = self.run(
            adjoint_totals,
            [self.value, self.grad, self.gain, (stats, shared((SUB, self.tokens))), self.z,
             self.mixed_out, self.mixed, self.step, self.age, self.picked, self.rates, self.span],
            [self.f32(self.tokens), self.low_out(), self.f32(SUB), self.f32(STATE), self.states_out()],
            [(self.tokens, GATES), self.wide, (self.tokens, LANE), (self.tokens, LANE)],
            after,
        )
        self.dmixed, self.back_part = (dmixed, self.long), (part, tile_of(self.states))
        return end, dz, side

    def back_grads(self, adjoint_in, after):
        direct, side, drates, dweight, dpicked = self.run(
            adjoint_grads,
            [self.step, self.mixed, self.age, self.dmixed, self.picked, self.rates, self.back_part, self.span,
             (adjoint_in, column(STATE)), self.kept, self.pre, self.step_w, self.skip],
            [self.f32(self.tokens), self.f32(SUB), self.f32(STATE), self.f32(SELECTED), self.picked_out()],
            [(self.tokens, GATES), self.wide, self.wide, self.states, self.wide, self.wide,
             (self.tokens, LANE), (self.tokens, LANE)],
            after,
        )
        self.direct = (direct, self.long)
        return side, drates, dweight, dpicked

    def last(self, dpicked, after):
        return self.run(
            last_mixer,
            self.conv + [(dpicked, self.picked_spec), self.direct, self.mixed],
            [self.low_out(), self.f32(2 * SUB), self.f32(SUB), self.f32(SELECTED)],
            [self.buffer, self.buffer],
            after,
        )


def over_rows(left_op, right_op):
    return lax.dot_general(
        left_op, right_op, (((0,), (0,)), ((), ())), preferred_element_type=jnp.float32
    )


def over_lanes(left_op, right_op):
    return lax.dot_general(
        left_op, right_op, (((1,), (1,)), ((), ())), preferred_element_type=jnp.float32
    )


def attend(repeats, query_ref, key_ref, value_ref, mask_ref, out_ref, total_ref):
    keys, values = key_ref[...], value_ref[...]
    for h in range(repeats):
        rows = slice(h * HD, (h + 1) * HD)
        scores = over_rows(keys, query_ref[rows, :]) + mask_ref[...]
        highest = jnp.max(scores, axis=0, keepdims=True)
        weights = jnp.exp(scores - highest)
        total = jnp.sum(weights, axis=0, keepdims=True)
        mixed = jnp.dot(values, weights.astype(jnp.bfloat16), preferred_element_type=jnp.float32)
        out_ref[rows, :] = mixed / total
        total_ref[0, h : h + 1, :] = highest + jnp.log(total)


def attend_back(
    repeats, query_ref, key_ref, value_ref, mask_ref, dout_ref, total_ref, delta_ref, place_ref,
    dquery_ref, dkey_ref, dvalue_ref,
):
    keys, values = key_ref[...], value_ref[...]
    reach = keys.shape[1] - META
    moved_to = pl.ds(pl.multiple_of(META + place_ref[0], LANE), reach)
    dkey_sum, dvalue_sum = 0.0, 0.0
    for h in range(repeats):
        rows = slice(h * HD, (h + 1) * HD)
        query, dout = query_ref[rows, :], dout_ref[rows, :]
        scores = over_rows(keys, query) + mask_ref[...]
        probs = jnp.exp(scores - total_ref[0, h : h + 1, :])
        dprobs = over_rows(values, dout)
        dscores = (probs * (dprobs - delta_ref[0, h : h + 1, :])).astype(jnp.bfloat16)
        probs = probs.astype(jnp.bfloat16)
        dquery_ref[rows, :] = jnp.dot(keys, dscores, preferred_element_type=jnp.float32)
        dkey_sum = dkey_sum + over_lanes(query, dscores)
        dvalue_sum = dvalue_sum + over_lanes(dout, probs)
    for target, found in ((dkey_ref, dkey_sum), (dvalue_ref, dvalue_sum)):
        target[...] = jnp.zeros_like(target)
        target[:, 0:META] = found[:, 0:META]
        target[:, moved_to] = found[:, META:]


def run_attention(query, keys, values, mask, after):
    count, reach = query.shape[1], keys.shape[1]
    tall = banded(HD * (H // KVH), count)
    stats = tile_of((SUB, count))
    keyed = banded(HD, reach)
    return run_tiles(
        functools.partial(attend, H // KVH),
        KVH,
        [(query, tall), (keys, keyed), (values, keyed), (mask, shared((reach, count)))],
        [(query.shape, jnp.float32, tall), ((KVH, SUB, count), jnp.float32, stats)],
        (),
        after,
    )


def run_attention_back(query, keys, values, mask, dout, totals, delta, place, spread, after):
    count, reach = query.shape[1], keys.shape[1]
    tall = banded(HD * (H // KVH), count)
    stats = tile_of((SUB, count))
    keyed = banded(HD, reach)
    found = ((keys.shape[0], spread), jnp.float32, banded(HD, spread))
    return run_tiles(
        functools.partial(attend_back, H // KVH),
        KVH,
        [
            (query, tall), (keys, keyed), (values, keyed), (mask, shared((reach, count))), (dout, tall),
            (totals, stats), (delta, stats), (place, pl.BlockSpec(memory_space=pltpu.SMEM)),
        ],
        [(query.shape, jnp.float32, tall), found, found],
        (),
        after,
    )


def dot_plain(left_op, right_op):
    return jnp.dot(left_op, right_op, preferred_element_type=jnp.float32)


def dot_left(left_op, right_op):
    return lax.dot_general(
        left_op, right_op, (((0,), (0,)), ((), ())), preferred_element_type=jnp.float32
    )


def dot_right(left_op, right_op):
    return lax.dot_general(
        left_op, right_op, (((1,), (1,)), ((), ())), preferred_element_type=jnp.float32
    )


def exact_dot(left_op, right_op):
    return jnp.dot(left_op, right_op, precision=HIGH, preferred_element_type=jnp.float32)


def exact_left(left_op, right_op):
    return lax.dot_general(
        left_op,
        right_op,
        (((0,), (0,)), ((), ())),
        precision=HIGH,
        preferred_element_type=jnp.float32,
    )


def exact_right(left_op, right_op):
    return lax.dot_general(
        left_op,
        right_op,
        (((1,), (1,)), ((), ())),
        precision=HIGH,
        preferred_element_type=jnp.float32,
    )


def low(values):
    return values.astype(jnp.bfloat16)


def wide(values):
    return values.astype(jnp.float32)


def swapped(values, axis):
    return straight(lax.ppermute(straight(values), axis, [(0, 1), (1, 0)]))


def moved(values, axis, distance):
    count = lax.axis_size(axis)
    route = [(i, i + distance) for i in range(count) if 0 <= i + distance < count]
    return lax.ppermute(values, axis, route)


def joined(mine, other, place):
    which = lax.broadcasted_iota(jnp.int32, (2,) + (1,) * mine.ndim, 0)
    both = jnp.where(which == place, mine[None], other[None])
    return both.reshape((2 * mine.shape[0],) + mine.shape[1:])


def chosen(pieces, place):
    result = pieces[0]
    for index, piece in enumerate(pieces[1:], 1):
        result = jnp.where(place == index, piece, result)
    return result


def pieces_of(values, count, axis):
    size = values.shape[axis] // count
    return [lax.slice_in_dim(values, i * size, (i + 1) * size, axis=axis) for i in range(count)]


def group_total(values):
    over_cols = values + swapped(values, "col")
    return over_cols + swapped(over_cols, "row")


def straight(values):
    return with_layout_constraint(values, Layout(tuple(range(values.ndim))))


def kept_apart(values, place, size, axis=0):
    mine = lax.dynamic_slice_in_dim(values, place * size, size, axis=axis)
    away = lax.dynamic_slice_in_dim(values, (1 - place) * size, size, axis=axis)
    return mine, away


class SeqSum:

    def __init__(self, left, right, scale=1.0, flip=False, after=()):
        self.count, self.place = lax.axis_size("seq"), lax.axis_index("seq")
        self.bits = self.count.bit_length() - 1
        self.right, self.scale, self.flip = right, scale, flip
        self.rows = left.shape[0] // self.count
        left = left.reshape((self.count, self.rows) + left.shape[1:])
        left = jnp.pad(left, ((0, 0), (0, -self.rows % 8), (0, 0)))
        self.left = left.reshape((2,) * self.bits + left.shape[1:])
        self.stage = 0
        self.send(low(self.product(self.half(self.left, True, after))))

    def half(self, values, away, after=()):
        bit = (self.place // 2**self.stage) % 2
        which = (1 - bit if away else bit) + nothing(*after)
        return lax.dynamic_index_in_dim(
            values, which, self.bits - 1 - self.stage, keepdims=False
        )

    def product(self, left):
        operands = (self.right, left) if self.flip else (left, self.right)
        dims = ((operands[0].ndim - 1,), (operands[1].ndim - 1,))
        found = lax.dot_general(
            *operands, (dims, ((), ())), preferred_element_type=jnp.float32
        )
        return self.scale * (jnp.moveaxis(found, 0, -2) if self.flip else found)

    def send(self, values):
        self.sent = straight(values)
        route = [(i, i ^ 2**self.stage) for i in range(self.count)]
        self.got = straight(lax.ppermute(self.sent, "seq", route))

    def step(self, *after):
        if self.stage == 0:
            mine = self.product(self.half(self.left, False, after))
        else:
            mine = wide(self.half(self.now, False, after))
        total = mine + wide(self.got)
        self.stage += 1
        if self.stage == self.bits:
            self.total = total
        else:
            self.now = straight(low(total))
            self.send(self.half(self.now, True))
        return self

    def finish(self, *after):
        while self.stage < self.bits:
            self.step(*after)
        rows = self.rows
        return self.total[:, :rows] if self.flip else self.total[:rows]


def seq_reduce(values):
    count, place = lax.axis_size("seq"), lax.axis_index("seq")
    bits = count.bit_length() - 1
    parts = values.reshape((2,) * bits + (values.shape[0] // count,) + values.shape[1:])
    for stage in range(bits):
        bit = (place // 2**stage) % 2
        axis = bits - 1 - stage
        mine = lax.dynamic_index_in_dim(parts, bit, axis, keepdims=False)
        away = lax.dynamic_index_in_dim(parts, 1 - bit, axis, keepdims=False)
        route = [(i, i ^ 2**stage) for i in range(count)]
        parts = mine + wide(lax.ppermute(low(away), "seq", route))
    return parts


def told(values, axes):
    count = lax.axis_size(axes)
    return lax.all_to_all(
        jnp.broadcast_to(values[None], (count,) + values.shape), axes, split_axis=0, concat_axis=0
    )


def all_total(values):
    count = lax.axis_size(ALL)
    shares = lax.all_to_all(values.reshape(count, -1), ALL, split_axis=0, concat_axis=0, tiled=True)
    return told(jnp.sum(shares, axis=0), ALL).reshape(-1)


def turned(values, cosine, sine, back):
    heads = values.reshape((values.shape[0] // HD, 2, HD // 2) + values.shape[1:])
    first, second = heads[:, :1], heads[:, 1:]
    sine = -sine if back else sine
    turned_pair = [first * cosine - second * sine, second * cosine + first * sine]
    return jnp.concatenate(turned_pair, axis=1).reshape(values.shape)


def entering_state(ends, spans, rates, reverse):
    count, place = lax.axis_size("seq"), lax.axis_index("seq")
    state = jnp.zeros_like(ends[0])
    for k in range(count):
        at = count - 1 - k if reverse else k
        reached = at > place if reverse else at < place
        decay = jnp.exp2(rates * spans[at][None, :])
        state = jnp.where(reached, decay * state + ends[at], state)
    return state


def shards(
    hidden_in,
    grad_out,
    segment_ids,
    pre_gain,
    qkv_weight,
    mixer_in_weight,
    meta_cache,
    conv_weight,
    conv_bias,
    select_weight,
    step_weight,
    step_bias,
    log_rates,
    skip_gain,
    attn_gain,
    mixer_gain,
    attn_out_weight,
    mixer_out_weight,
    post_gain,
    gate_weight,
    up_weight,
    down_weight,
):
    row, col, seq = lax.axis_index("row"), lax.axis_index("col"), lax.axis_index("seq")
    tokens = hidden_in.shape[0]
    quarter = DI // 4
    half = D // 2
    lanes = -(-quarter // LANE) * LANE
    member = 2 * row + col

    def by_row(first, second):
        return jnp.where(row == 0, first, second)

    def row_joined(values):
        return joined(values, swapped(values, "row"), row)

    def col_joined(values):
        return joined(values, swapped(values, "col"), col)

    def col_summed(part):
        mine, away = kept_apart(part, col, part.shape[0] // 2)
        return mine + wide(swapped(low(away), "col"))

    def row_summed(part):
        part = low(part)
        return wide(part) + wide(swapped(part, "row"))

    def row_scattered(part):
        mine, away = kept_apart(part, row, part.shape[0] // 2)
        return mine + wide(swapped(low(away), "row"))

    def over_cols(values):
        return values + swapped(values, "col")

    hidden_m = row_joined(hidden_in.T)
    gains_m = row_joined(jnp.stack([pre_gain, post_gain], axis=1))
    pre_g, post_g = gains_m[:, :1], gains_m[:, 1:]
    hm = wide(hidden_m)
    pre_factor = lax.rsqrt(over_cols(jnp.sum(hm * hm, axis=0)) / D + EPS)[None, :]
    first_m = low(hm * pre_factor * pre_g)

    inner_part = straight(over_rows(mixer_in_weight, first_m))
    near, far = inner_part[: 2 * quarter], inner_part[2 * quarter :]
    near_m, near_away = kept_apart(near, col, quarter)
    far_m, far_away = kept_apart(far, col, quarter)
    give_m, keep_m = by_row(far_m, near_m), by_row(near_m, far_m)
    give_got = swapped(low(by_row(far_away, near_away)), "col")
    keep_got = swapped(low(by_row(near_away, far_away)), "col")
    given = low(give_m + wide(give_got))
    taken = swapped(given, "row")
    kept_in = low(keep_m + wide(keep_got))
    qkv_part = low(col_summed(over_rows(qkv_weight, first_m)))
    qkv_core = lax.all_to_all(qkv_part, GROUP, split_axis=1, concat_axis=0, tiled=True)
    def filled(values):
        return jnp.pad(values, ((0, lanes - quarter), (0, 0)))

    def channels(values, axis):
        part = chosen(pieces_of(values, 4, axis), member)
        sides = [(0, lanes - quarter) if i == axis else (0, 0) for i in range(values.ndim)]
        return jnp.pad(part, sides)

    inner_own = filled(by_row(kept_in, taken))
    gate_z = filled(by_row(taken, kept_in))

    own_tokens = tokens // 4
    devices_back = (WIN + own_tokens - 2) // own_tokens
    halo_rows = devices_back * own_tokens
    tail_rows = CONV - 1
    kv_width = KVH * HD
    start_row = seq * tokens + member * own_tokens
    seg_padded = jnp.concatenate([jnp.full((halo_rows,), -1, jnp.int32), segment_ids])
    key_segs = lax.dynamic_slice(seg_padded, (start_row,), (halo_rows + own_tokens,))
    query_segs = key_segs[halo_rows:]
    query_glob = start_row + jnp.arange(own_tokens, dtype=jnp.int32)
    key_glob = start_row - halo_rows + jnp.arange(halo_rows + own_tokens, dtype=jnp.int32)
    doc_start = jnp.sum((segment_ids[:, None] < query_segs[None, :]).astype(jnp.int32), axis=0)
    frequency = THETA ** (-2.0 * jnp.arange(HD // 2, dtype=jnp.float32) / HD)
    angles = frequency[:, None] * wide(query_glob - doc_start)[None, :]
    cosine, sine = jnp.cos(angles), jnp.sin(angles)
    score_scale = HD ** (-0.5)
    query = low(turned(wide(qkv_core[:D]), cosine, sine, False) * score_scale)
    key_own = low(turned(wide(qkv_core[D : D + kv_width]), cosine, sine, False))
    pair_own = jnp.concatenate([key_own, qkv_core[D + kv_width :]], axis=0)
    groups_back = (WIN + tokens - 2) // tokens
    distance = query_glob[None, :] - key_glob[:, None]
    visible = (key_segs[:, None] == query_segs[None, :]) & (distance >= 0) & (distance < WIN)
    mask = jnp.where(
        jnp.concatenate([jnp.ones((META, own_tokens), jnp.bool_), visible], axis=0), 0.0, NEG
    )

    conv_w, conv_b = channels(conv_weight, 1), channels(conv_bias, 0)
    select_w, step_w = channels(select_weight.T, 1), channels(step_weight, 1)
    step_b, skip_g = channels(step_bias, 0), channels(skip_gain, 0)
    mixer_g = channels(mixer_gain, 0)
    decay_rates = jnp.exp(channels(log_rates, 0).T)
    valid = lax.broadcasted_iota(jnp.int32, (1, lanes), 1) < quarter
    rates = jnp.where(valid, -LOG2E * decay_rates, 0.0)

    edge = wide(inner_own[:, tokens - LANE :])[:, LANE - tail_rows :].T
    tail = jnp.pad(moved(edge, "seq", 1), ((SUB - tail_rows, 0), (0, 0)))
    conv_segs = lax.dynamic_slice(
        seg_padded, (seq * tokens + halo_rows - tail_rows,), (tokens + tail_rows,)
    )
    own_segs = conv_segs[tail_rows:]
    age = sum(wide(conv_segs[tap : tap + tokens] == own_segs) for tap in range(tail_rows))
    age = jnp.broadcast_to(age[:, None], (tokens, LANE))
    step_w = jnp.pad(step_w, ((0, SELECTED - DT_RANK), (0, 0)))
    mixer = Mixer(
        tokens, lanes, age, inner_own, tail, gate_z, conv_w, conv_b[None], select_w, step_w, step_b[None],
        rates, skip_g[None], mixer_g[None],
    )
    mixed_in, picked = mixer.first()
    pairs = told(pair_own, GROUP)
    pair_group = jnp.concatenate(
        [
            lax.dynamic_index_in_dim(pairs, i + nothing(mixed_in), 0, keepdims=False)
            for i in range(pairs.shape[0])
        ],
        axis=1,
    )
    halo = [moved(pair_group, "seq", offset) for offset in range(groups_back, 0, -1)]
    skipped = (groups_back * tokens - halo_rows) + member * own_tokens
    window = lax.dynamic_slice_in_dim(
        jnp.concatenate(halo + [pair_group], axis=1), skipped, halo_rows + own_tokens, axis=1
    )
    meta_pair = meta_cache.transpose(0, 2, 1).reshape(2 * kv_width, META)
    pair_all = jnp.concatenate([meta_pair, window], axis=1)
    selected = group_total(picked)
    attn, log_totals = run_attention(query, pair_all[:kv_width], pair_all[kv_width:], mask, ())
    end = mixer.totals(selected, (attn,))
    ends = told(end, "seq")
    spans = ends[:, STATE, :]
    state_in = entering_state(ends[:, :STATE], spans, rates, False)

    attn_factor = lax.rsqrt(jnp.mean(attn * attn, axis=0, keepdims=True) + EPS)
    attn_low = low(attn * attn_factor * attn_gain[:, None])
    attn_part = lax.all_to_all(attn_low, GROUP, split_axis=0, concat_axis=1, tiled=True)
    attn_rows = col_joined(attn_part)
    grad_m = row_joined(grad_out.T)
    down_t, mixer_out_t = down_weight.T, mixer_out_weight.T
    dact = col_summed(over_rows(down_t, grad_m))

    squares = mixer.outputs(state_in, (attn_rows, dact))
    mixer_factor = lax.rsqrt(group_total(squares) / DI + EPS)
    mixer_rows = col_joined(mixer.normed(mixer_factor, mixer_g)[:quarter])

    mix_m = row_summed(
        0.5 * (over_rows(attn_out_weight, attn_rows) + dot_plain(mixer_out_t, mixer_rows))
    )
    resid_m = hm + mix_m
    post_factor = lax.rsqrt(over_cols(jnp.sum(resid_m * resid_m, axis=0)) / D + EPS)[None, :]
    second_m = low(resid_m * post_factor * post_g)
    gate_act = col_summed(over_rows(gate_weight, second_m))
    up_act = col_summed(over_rows(up_weight, second_m))
    sig_gate = jax.nn.sigmoid(gate_act)
    dgate_low = low(dact * up_act * sig_gate * (1.0 + gate_act * (1.0 - sig_gate)))
    dup_low = low(dact * gate_act * sig_gate)
    act_low = low(gate_act * sig_gate * up_act)
    dgate_rows = col_joined(dgate_low)
    dup_rows = col_joined(dup_low)
    act_rows = col_joined(act_low)
    dsecond_m = row_summed(dot_plain(gate_weight, dgate_rows) + dot_plain(up_weight, dup_rows))
    sum_gate = SeqSum(dgate_rows, second_m, 1.0, True)
    sum_up = SeqSum(dup_rows, second_m, 1.0, True)
    weighted_m = dsecond_m * post_g
    inner_sum = over_cols(jnp.sum(weighted_m * resid_m, axis=0)) / D
    pull_back = post_factor**3 * inner_sum[None, :]
    dmid_m = wide(grad_m) + post_factor * weighted_m - resid_m * pull_back
    post_part = jnp.sum(dsecond_m * resid_m * post_factor, axis=1)
    low_m = low(dmid_m)

    dmixer_low = filled(low(0.5 * col_summed(over_rows(mixer_out_t, low_m))))
    dattn_part = low(0.5 * col_summed(dot_plain(attn_out_weight, low_m)))
    dattn_core = lax.all_to_all(dattn_part, GROUP, split_axis=1, concat_axis=0, tiled=True)

    mixer_sum = group_total(mixer.norm_pull(dmixer_low)) / DI
    back_end, dz_own, side_norm = mixer.back_totals(
        mixer_factor,
        mixer_factor**3 * mixer_sum,
        [sum_gate.sent, sum_up.sent],
    )
    adjoint_in = entering_state(told(back_end, "seq"), spans, rates, True)

    incoming = wide(dattn_core)
    attn_weighted = incoming * attn_gain[:, None]
    attn_sum = jnp.mean(attn_weighted * attn, axis=0, keepdims=True)
    dattn = low(attn_factor * attn_weighted - attn * (attn_factor**3 * attn_sum))
    attn_gain_part = jnp.sum(incoming * attn * attn_factor, axis=1)
    delta = jnp.sum((wide(dattn) * attn).reshape(H, HD, own_tokens), axis=1)
    delta = jnp.pad(
        delta.reshape(KVH, H // KVH, own_tokens), ((0, 0), (0, SUB - H // KVH), (0, 0))
    )
    reach = groups_back * tokens
    dquery, dkey, dvalue = run_attention_back(
        query, pair_all[:kv_width], pair_all[kv_width:], mask, dattn, log_totals, delta,
        skipped.reshape((1,)), META + reach + tokens,
        [back_end, sum_gate.got],
    )
    sum_gate.step(dquery)
    sum_up.step(sum_gate.now)

    sum_down = SeqSum(grad_m, act_rows, 1.0, False, [adjoint_in])
    both_rows = jnp.concatenate([attn_rows, mixer_rows], axis=0)
    sum_out = SeqSum(low_m, both_rows, 0.5, False, [adjoint_in])
    side_step, drates, step_weight_part, dpicked = mixer.back_grads(
        adjoint_in,
        [sum_gate.now, sum_up.now, sum_down.sent, sum_out.sent],
    )
    dpicked = held_until(dpicked, [sum_gate.got, sum_up.got, sum_down.got, sum_out.got])
    sums = [sum_gate, sum_up, sum_out, sum_down]
    for part in sums:
        part.step(drates)
    dinner_own, edges, side_conv, select_part = mixer.last(
        group_total(dpicked),
        [sum_gate.got, sum_up.got],
    )
    held = wide(nothing(drates))
    dgroup = jnp.concatenate([dkey[:, META + reach :], dvalue[:, META + reach :]], axis=0)
    dgroup = dgroup + wide(nothing(select_part))
    for offset in range(1, groups_back + 1):
        at = slice(META + reach - offset * tokens, META + reach - (offset - 1) * tokens)
        piece = low(jnp.concatenate([dkey[:, at], dvalue[:, at]], axis=0) + held)
        dgroup = dgroup + wide(moved(piece, "seq", -offset))
    shares = lax.all_to_all(
        low(dgroup).reshape(2 * kv_width, 4, own_tokens), GROUP, split_axis=1, concat_axis=1
    )
    dpair_own = jnp.sum(wide(shares), axis=1)
    dquery = turned(dquery * score_scale, cosine, sine, True)
    dkey_own = turned(dpair_own[:kv_width], cosine, sine, True)
    dqkv_core = low(
        jnp.concatenate([dquery, dkey_own, dpair_own[kv_width:]], axis=0)
    )
    dqkv_part = lax.all_to_all(dqkv_core, GROUP, split_axis=0, concat_axis=1, tiled=True)
    dqkv_rows = col_joined(dqkv_part)
    sum_qkv = SeqSum(dqkv_rows, first_m)

    lost = moved(edges[SUB - tail_rows : SUB], "seq", -1)
    ending = low(edges[2 * SUB - tail_rows :] + lost).T
    dinner_own = lax.dynamic_update_slice(dinner_own, ending, (0, tokens - tail_rows))[:quarter]
    dz_t = dz_own[:quarter]
    got_back = swapped(by_row(dz_t, dinner_own), "row")
    dnear = col_joined(by_row(dinner_own, got_back))
    dfar = col_joined(by_row(got_back, dz_t))
    dinner_rows = jnp.concatenate([dnear, dfar], axis=0)
    dchunks = dinner_rows.reshape(lax.axis_size("seq"), -1, tokens)
    cut = dchunks.shape[1] // 16 * 8
    sum_out.step(select_part)
    sum_down.step(select_part)
    sums_in = [
        SeqSum(dchunks[:, :cut].reshape(-1, tokens), first_m, 1.0, False, [sum_out.got]),
        SeqSum(dchunks[:, cut:].reshape(-1, tokens), first_m),
    ]
    begun = [part.sent for part in sums_in]
    params = jnp.concatenate(
        [
            select_part,
            step_weight_part[:DT_RANK],
            drates,
            side_conv[: CONV + 1],
            side_step[:1] + wide(nothing(*begun)),
            side_norm[:2],
        ],
        axis=0,
    )
    params = seq_reduce(low(params))
    params = wide(told(low(params), ALL))
    count = lax.axis_size("seq")
    params = params.reshape((count, 4) + params.shape[1:])
    params = jnp.concatenate(
        [params[:, q].reshape(-1, lanes)[:, :quarter] for q in range(4)], axis=1
    )

    dqkv_late = lax.dynamic_slice_in_dim(dqkv_rows, nothing(*begun), dqkv_rows.shape[0], axis=0)
    dfirst_part = dot_plain(qkv_weight, dqkv_late) + dot_plain(mixer_in_weight, dinner_rows)
    first_sum = group_total(jnp.sum(dfirst_part * pre_g * hm, axis=0)) / D

    def block(values):
        return lax.dynamic_slice_in_dim(values, row * (half // 2), half // 2, axis=0)

    dfirst = row_scattered(dfirst_part)
    own_hidden = block(hm)
    grad_in = (
        block(dmid_m)
        + pre_factor * dfirst * block(pre_g)
        - own_hidden * (pre_factor**3 * first_sum[None, :])
    )
    pre_part = jnp.sum(dfirst * own_hidden * pre_factor, axis=1)
    act_late = lax.dynamic_slice_in_dim(act_rows, nothing(*begun), act_rows.shape[0], axis=0)
    hidden_out = low(block(resid_m) + row_scattered(dot_plain(down_t, act_late)))

    gain_block = pre_gain.shape[0]
    block_pos = (2 * col + row) * gain_block

    def spread(part):
        return lax.dynamic_update_slice(jnp.zeros((D,), jnp.float32), part, (block_pos,))

    early = all_total(
        jnp.concatenate(
            [
                (dkey[:, :META] + wide(nothing(*begun))).reshape(-1),
                dvalue[:, :META].reshape(-1),
                attn_gain_part,
                spread(block(post_part[:, None])[:, 0]),
            ]
        )
    )
    meta_size = 2 * kv_width * META
    meta_grad = early[:meta_size].reshape(2, kv_width, META).transpose(0, 2, 1)
    attn_gain_grad = early[meta_size : meta_size + D]
    post_grad = early[meta_size + D :]
    pre_parts = told(pre_part, ALL).reshape((count, 2, 2, gain_block))
    pre_grad = jnp.sum(pre_parts, axis=0).transpose(1, 0, 2).reshape(-1)
    out_grads = sum_out.finish(*begun)
    for part in sums_in + sums_in + [sum_qkv]:
        part.step(*begun)
    ranks = DT_RANK + 2 * STATE
    at_rates = ranks + DT_RANK
    at_conv = at_rates + STATE
    return (
        hidden_out.T,
        grad_in.T,
        pre_grad,
        sum_qkv.finish(*begun).T,
        jnp.concatenate([piece.finish(params) for piece in sums_in], axis=0).T,
        meta_grad,
        params[at_conv : at_conv + CONV],
        params[at_conv + CONV],
        params[:ranks].T,
        params[ranks:at_rates],
        params[at_conv + CONV + 1],
        params[at_rates:at_conv].T,
        params[at_conv + CONV + 2],
        attn_gain_grad,
        params[at_conv + CONV + 3],
        out_grads[:, :half].T,
        out_grads[:, half:].T,
        post_grad,
        sum_gate.finish(*begun),
        sum_up.finish(*begun),
        sum_down.finish(*begun).T,
    )


def solution(mesh):
    in_specs = (
        P("seq", ("col", "row")),
        P("seq", ("col", "row")),
        P(),
        P(("col", "row")),
        P("col", "row"),
        P("col", "row"),
        P(),
        P(),
        P(),
        P(),
        P(),
        P(),
        P(),
        P(),
        P(),
        P(),
        P("row", "col"),
        P("row", "col"),
        P(("col", "row")),
        P("col", "row"),
        P("col", "row"),
        P("row", "col"),
    )
    out_specs = (
        P("seq", ("col", "row")),
        P("seq", ("col", "row")),
        P(),
        P("col", ("row", "seq")),
        P("col", ("row", "seq")),
        P(),
        P(),
        P(),
        P(),
        P(),
        P(),
        P(),
        P(),
        P(),
        P(),
        P("row", ("col", "seq")),
        P("row", ("col", "seq")),
        P(),
        P("col", ("row", "seq")),
        P("col", ("row", "seq")),
        P("row", ("col", "seq")),
    )
    return jax.shard_map(shards, mesh=mesh, in_specs=in_specs, out_specs=out_specs, check_vma=False)
```

```python
import functools
import math

import jax
import jax.numpy as jnp
from jax import lax
from jax.experimental import pallas as pl
from jax.experimental.layout import Layout, with_layout_constraint
from jax.experimental.pallas import tpu as pltpu
from jax.sharding import PartitionSpec as P

D = 1600
H = 25
KVH = 5
HD = 64
DI = 3200
STATE = 16
DT_RANK = 100
CONV = 4
META = 128
WIN = 1024


EPS = 1e-05
NEG = -1e30
THETA = 10000.0
HIGH = lax.Precision.HIGHEST
ALL = ("seq", "row", "col")
GROUP = ("row", "col")
LOG2E = 1.4426950408889634
LN2 = 0.6931471805599453
FAR = 1e30
SUB = 8
LANE = 128
TAIL = CONV - 1
GATES = 2 * STATE
SELECTED = DT_RANK + GATES
VMEM_ASK = 58 * 2**20
SMALL = pl.CostEstimate(flops=1024, transcendentals=0, bytes_accessed=1024)


def nothing(*after, since=None):
    total = 0.0
    for values in after:
        start = (0,) * values.ndim
        if since is not None:
            start = (since,) + start[1:]
        corner = lax.dynamic_slice(values, start, (1,) * values.ndim)
        total = total + jnp.abs(corner.astype(jnp.float32).reshape(()))
    return jnp.minimum(jnp.float32(total), 0.0).astype(jnp.int32)


def exact(left_op, right_op, left_dim, right_dim):
    return lax.dot_general(
        left_op,
        right_op,
        (((left_dim,), (right_dim,)), ((), ())),
        precision=HIGH,
        preferred_element_type=jnp.float32,
    )


def gate_places():
    shape = (GATES, SELECTED)
    found = lax.broadcasted_iota(jnp.int32, shape, 1) - lax.broadcasted_iota(jnp.int32, shape, 0)
    return (found == DT_RANK).astype(jnp.float32)


def token_row(values):
    return exact(jnp.ones((SUB, LANE), jnp.float32), values, 1, 1)


def upright(ref):
    return ref[...].astype(jnp.float32).T


def spread_gates(source, length, *targets):

    def one(t, carry):
        rows = source[pl.ds(t, SUB, stride=length), :]
        for low, target in targets:
            for n in range(STATE):
                column = rows[:, low + n : low + n + 1]
                target[t * STATE + n] = jnp.broadcast_to(column, (SUB, LANE))
        return carry

    lax.fori_loop(0, length, one, 0)


def chunk_decay(rate_ref, total_row):
    return jnp.exp2(rate_ref[...] * total_row)


def convolved(inner_ref, tail_ref, age_ref, weight_ref, bias_ref, padded):
    total = inner_ref.shape[1]
    padded[0:SUB, :] = tail_ref[...]
    padded[SUB : SUB + total, :] = upright(inner_ref)
    result = jnp.broadcast_to(bias_ref[...], (total, LANE))
    for tap in range(CONV):
        found = padded[SUB - TAIL + tap : SUB - TAIL + tap + total, :]
        if tap < TAIL:
            found = jnp.where(age_ref[...] >= TAIL - tap, found, 0.0)
        result = result + weight_ref[tap : tap + 1, :] * found
    return result


def first_mixer(inner_ref, tail_ref, age_ref, weight_ref, bias_ref, select_ref, mixed_ref, picked_ref, padded):
    conv = convolved(inner_ref, tail_ref, age_ref, weight_ref, bias_ref, padded)
    mixed = conv * jax.nn.sigmoid(conv)
    mixed_ref[...] = mixed
    part = exact(mixed, select_ref[...], 1, 1)

    @pl.when(pl.program_id(0) == 0)
    def _():
        picked_ref[...] = part

    @pl.when(pl.program_id(0) > 0)
    def _():
        picked_ref[...] += part


def lapse_of(age_ref, rows, step):
    return jnp.where(age_ref[rows, :] > 0.0, step, FAR)


def scan_totals(
    picked_ref, mixed_ref, age_ref, weight_ref, bias_ref, rate_ref,
    step_ref, pre_ref, end_ref, part_ref, span_ref, gates, wide,
):
    length = mixed_ref.shape[0] // SUB

    @pl.when(pl.program_id(0) == 0)
    def _():
        gates[...] = exact(picked_ref[...], gate_places(), 1, 1)
        spread_gates(gates, length, (0, wide))

    pre = exact(picked_ref[...], weight_ref[...], 1, 0) + bias_ref[...]
    pre_ref[...] = pre
    step_ref[...] = jnp.maximum(pre, 0.0) + jnp.log1p(jnp.exp(-jnp.abs(pre)))
    rates = [jnp.broadcast_to(rate_ref[n : n + 1, :], (SUB, LANE)) for n in range(STATE)]

    def one(t, carry):
        states, span = carry
        rows = pl.ds(t, SUB, stride=length)
        step = step_ref[rows, :]
        lapse = lapse_of(age_ref, rows, step)
        push = step * mixed_ref[rows, :]
        states = tuple(
            jnp.exp2(lapse * rates[n]) * states[n] + push * wide[t * STATE + n] for n in range(STATE)
        )
        return (states, span + lapse)

    zero = jnp.zeros((SUB, LANE), jnp.float32)
    states, span = lax.fori_loop(0, length, one, ((zero,) * STATE, zero), unroll=2)
    for n in range(STATE):
        part_ref[0, n] = states[n]
    span_ref[...] = span
    total = jnp.zeros((STATE, LANE), jnp.float32)
    lapsed = jnp.zeros((1, LANE), jnp.float32)
    for k in range(SUB):
        here = span_ref[k : k + 1, :]
        total = chunk_decay(rate_ref, here) * total + part_ref[0, :, k, :]
        lapsed = lapsed + here
    end_ref[0:STATE, :] = total
    end_ref[STATE:, :] = jnp.broadcast_to(lapsed, (SUB, LANE))


def scan_outputs(
    step_ref, mixed_ref, age_ref, picked_ref, rate_ref, part_ref, span_ref, start_ref, skip_ref, z_ref,
    mixed_out_ref, value_ref, square_ref, kept_ref, gates, wide, wide_read, squares,
):
    length = mixed_ref.shape[0] // SUB

    @pl.when(pl.program_id(0) == 0)
    def _():
        gates[...] = exact(picked_ref[...], gate_places(), 1, 1)
        spread_gates(gates, length, (0, wide), (STATE, wide_read))
        squares[...] = jnp.zeros_like(squares)

    state = start_ref[...]
    for k in range(SUB):
        kept_ref[0, 0:STATE, k, :] = state
        state = chunk_decay(rate_ref, span_ref[k : k + 1, :]) * state + part_ref[0, :, k, :]
    rates = [jnp.broadcast_to(rate_ref[n : n + 1, :], (SUB, LANE)) for n in range(STATE)]

    def one(t, states):
        rows = pl.ds(t, SUB, stride=length)
        step = step_ref[rows, :]
        lapse = lapse_of(age_ref, rows, step)
        push = step * mixed_ref[rows, :]
        new = []
        seen = [None, None]
        for n in range(STATE):
            value = jnp.exp2(lapse * rates[n]) * states[n] + push * wide[t * STATE + n]
            kept_ref[0, (t + 1) * STATE + n] = value
            part = value * wide_read[t * STATE + n]
            seen[n % 2] = part if seen[n % 2] is None else seen[n % 2] + part
            new.append(value)
        mixed_out_ref[rows, :] = seen[0] + seen[1]
        return tuple(new)

    lax.fori_loop(0, length, one, tuple(kept_ref[0, n] for n in range(STATE)), unroll=2)
    mixed_out = mixed_out_ref[...] + skip_ref[...] * mixed_ref[...]
    mixed_out_ref[...] = mixed_out
    z = upright(z_ref)
    value = mixed_out * z * jax.nn.sigmoid(z)
    value_ref[...] = value
    squares[...] += value * value

    @pl.when(pl.program_id(0) == pl.num_programs(0) - 1)
    def _():
        square_ref[...] = token_row(squares[...])


def normed(value_ref, factor_ref, gain_ref, out_ref):
    out_ref[...] = (value_ref[...].T * factor_ref[0:1, :] * gain_ref[...]).astype(out_ref.dtype)


def norm_pull(value_ref, grad_ref, gain_ref, sum_ref, sums):
    part = upright(grad_ref) * gain_ref[...] * value_ref[...]

    @pl.when(pl.program_id(0) == 0)
    def _():
        sums[...] = part

    @pl.when(pl.program_id(0) > 0)
    def _():
        sums[...] += part

    @pl.when(pl.program_id(0) == pl.num_programs(0) - 1)
    def _():
        sum_ref[...] = token_row(sums[...])


def adjoint_totals(
    value_ref, grad_ref, gain_ref, stats_ref, z_ref, mixed_out_ref, mixed_ref,
    step_ref, age_ref, picked_ref, rate_ref, span_ref,
    dmixed_ref, dz_ref, side_ref, end_ref, part_ref, gates, wide, factors, pulls,
):
    total = mixed_ref.shape[0]
    length = total // SUB

    @pl.when(pl.program_id(0) == 0)
    def _():
        gates[...] = exact(picked_ref[...], gate_places(), 1, 1)
        spread_gates(gates, length, (STATE, wide))
        columns = stats_ref[...].T
        factors[...] = jnp.broadcast_to(columns[:, 0:1], (total, LANE))
        pulls[...] = jnp.broadcast_to(columns[:, 1:2], (total, LANE))

    grad, z, value = upright(grad_ref), upright(z_ref), value_ref[...]
    dvalue = factors[...] * gain_ref[...] * grad - value * pulls[...]
    sig = jax.nn.sigmoid(z)
    dmixed = dvalue * z * sig
    dmixed_ref[...] = dmixed
    dz = dvalue * mixed_out_ref[...] * sig * (1.0 + z * (1.0 - sig))
    dz_ref[...] = dz.T.astype(dz_ref.dtype)
    side_ref[...] = jnp.zeros_like(side_ref)
    side_ref[0:1, :] = jnp.sum(dmixed * mixed_ref[...], axis=0, keepdims=True)
    side_ref[1:2, :] = jnp.sum(grad * value * factors[...], axis=0, keepdims=True)
    rates = [jnp.broadcast_to(rate_ref[n : n + 1, :], (SUB, LANE)) for n in range(STATE)]

    def one(k, carry):
        t = length - 1 - k
        rows = pl.ds(t, SUB, stride=length)
        lapse = lapse_of(age_ref, rows, step_ref[rows, :])
        dout = dmixed_ref[rows, :]
        return tuple(
            jnp.exp2(lapse * rates[n]) * (carry[n] + dout * wide[t * STATE + n]) for n in range(STATE)
        )

    zero = jnp.zeros((SUB, LANE), jnp.float32)
    carry = lax.fori_loop(0, length, one, (zero,) * STATE, unroll=2)
    for n in range(STATE):
        part_ref[0, n] = carry[n]
    ends = jnp.zeros((STATE, LANE), jnp.float32)
    for k in reversed(range(SUB)):
        ends = chunk_decay(rate_ref, span_ref[k : k + 1, :]) * ends + part_ref[0, :, k, :]
    end_ref[...] = ends


def adjoint_grads(
    step_ref, mixed_ref, age_ref, dout_ref, picked_ref, rate_ref, part_ref, span_ref, start_ref, kept_ref,
    pre_ref, weight_ref, skip_ref,
    direct_ref, side_ref, drate_ref, dweight_ref, dpicked_ref,
    gates, wide, wide_read, entry, dgate_ref, dread_ref, dprod_ref, dstep_ref,
):
    length = mixed_ref.shape[0] // SUB

    @pl.when(pl.program_id(0) == 0)
    def _():
        gates[...] = exact(picked_ref[...], gate_places(), 1, 1)
        spread_gates(gates, length, (0, wide), (STATE, wide_read))
        dgate_ref[...] = jnp.zeros_like(dgate_ref)
        dread_ref[...] = jnp.zeros_like(dread_ref)

    state = start_ref[...]
    for k in reversed(range(SUB)):
        entry[:, k, :] = state
        state = chunk_decay(rate_ref, span_ref[k : k + 1, :]) * state + part_ref[0, :, k, :]
    half = STATE // 2
    zero = jnp.zeros((SUB, LANE), jnp.float32)
    for low in (0, half):
        rates = [jnp.broadcast_to(rate_ref[n : n + 1, :], (SUB, LANE)) for n in range(low, low + half)]

        def one(j, carry, low=low, rates=rates):
            incoming, rate_sum = carry
            t = length - 1 - j
            rows = pl.ds(t, SUB, stride=length)
            step = step_ref[rows, :]
            lapse = lapse_of(age_ref, rows, step)
            push = step * mixed_ref[rows, :]
            dout = dout_ref[rows, :]
            outgoing, sums = [], []
            dprod, dstep = zero, zero
            for i in range(half):
                at = t * STATE + low + i
                adjoint = incoming[i] + dout * wide_read[at]
                dread_ref[at] = dread_ref[at] + kept_ref[0, at + STATE] * dout
                dgate_ref[at] = dgate_ref[at] + adjoint * push
                dprod = dprod + adjoint * wide[at]
                passed = jnp.exp2(lapse * rates[i]) * adjoint
                pull = passed * kept_ref[0, at]
                dstep = dstep + pull * rates[i]
                sums.append(rate_sum[i] + pull * step)
                outgoing.append(passed)
            if low == 0:
                dprod_ref[rows, :] = dprod
                dstep_ref[rows, :] = dstep
            else:
                dprod_ref[rows, :] = dprod_ref[rows, :] + dprod
                dstep_ref[rows, :] = (dstep_ref[rows, :] + dstep) * LN2
            return (tuple(outgoing), tuple(sums))

        start = (tuple(entry[low + i] for i in range(half)), (zero,) * half)
        _, rate_sum = lax.fori_loop(0, length, one, start)
        for i in range(half):
            found = jnp.sum(rate_sum[i], axis=0, keepdims=True)
            drate_ref[low + i : low + i + 1, :] = found * rate_ref[low + i : low + i + 1, :] * LN2

    dprod = dprod_ref[...]
    direct_ref[...] = dout_ref[...] * skip_ref[...] + dprod * step_ref[...]
    dpre = (dstep_ref[...] + dprod * mixed_ref[...]) * jax.nn.sigmoid(pre_ref[...])
    side_ref[...] = jnp.broadcast_to(jnp.sum(dpre, axis=0, keepdims=True), (SUB, LANE))
    dweight_ref[...] = exact(picked_ref[...], dpre, 0, 0)
    part = exact(dpre, weight_ref[...], 1, 1)

    @pl.when(pl.program_id(0) == 0)
    def _():
        dpicked_ref[...] = part

    @pl.when(pl.program_id(0) > 0)
    def _():
        dpicked_ref[...] += part

    @pl.when(pl.program_id(0) == pl.num_programs(0) - 1)
    def _():
        place = lax.broadcasted_iota(jnp.int32, (SUB, GATES), 1)

        def gather(t, carry):
            found = jnp.zeros((SUB, GATES), jnp.float32)
            for base, source in ((0, dgate_ref), (STATE, dread_ref)):
                for n in range(STATE):
                    summed = jnp.sum(source[t * STATE + n], axis=1, keepdims=True)
                    found = jnp.where(place == base + n, summed, found)
            gates[pl.ds(t, SUB, stride=length), :] = found
            return carry

        lax.fori_loop(0, length, gather, 0)
        dpicked_ref[...] += exact(gates[...], gate_places(), 1, 0)


def last_mixer(
    inner_ref, tail_ref, age_ref, weight_ref, bias_ref, select_ref, dpicked_ref, direct_ref, mixed_ref,
    dinner_ref, edge_ref, side_ref, dselect_ref, padded, spilled,
):
    total = mixed_ref.shape[0]
    conv = convolved(inner_ref, tail_ref, age_ref, weight_ref, bias_ref, padded)
    sig = jax.nn.sigmoid(conv)
    dmixed = direct_ref[...] + exact(dpicked_ref[...], select_ref[...], 1, 0)
    dconv = dmixed * sig * (1.0 + conv * (1.0 - sig))
    dselect_ref[...] = exact(dpicked_ref[...], mixed_ref[...], 0, 0)
    side_ref[...] = jnp.zeros_like(side_ref)
    side_ref[CONV : CONV + 1, :] = jnp.sum(dconv, axis=0, keepdims=True)
    spilled[...] = jnp.zeros_like(spilled)
    for tap in range(CONV):
        at = slice(SUB - TAIL + tap, SUB - TAIL + tap + total)
        masked = dconv
        if tap < TAIL:
            masked = jnp.where(age_ref[...] >= TAIL - tap, dconv, 0.0)
        side_ref[tap : tap + 1, :] = jnp.sum(masked * padded[at, :], axis=0, keepdims=True)
        spilled[at, :] += masked * weight_ref[tap : tap + 1, :]
    edge_ref[0:SUB, :] = spilled[0:SUB, :]
    edge_ref[SUB:, :] = spilled[total : total + SUB, :]
    dinner_ref[...] = spilled[SUB:, :].T.astype(dinner_ref.dtype)


def column(rows):
    return pl.BlockSpec((rows, LANE), lambda i: (0, i))


def banded(rows, width):
    return pl.BlockSpec((rows, width), lambda i: (i, 0))


def shared(shape):
    return pl.BlockSpec(shape, lambda i: (0,) * len(shape))


def tile_of(shape):
    return pl.BlockSpec((1,) + shape, lambda i: (i,) + (0,) * len(shape))


def run_tiles(body, steps, ins, outs, scratch=(), after=()):
    args = [value for value, _ in ins]
    specs = [spec for _, spec in ins]
    args = args + list(after)
    specs = specs + [pl.BlockSpec(memory_space=pl.ANY)] * len(after)

    def kernel(*refs):
        body(*refs[: len(ins)], *refs[len(args) :])

    return pl.pallas_call(
        kernel,
        grid=(steps,),
        in_specs=specs,
        out_specs=[spec for _, _, spec in outs],
        out_shape=[jax.ShapeDtypeStruct(shape, dtype) for shape, dtype, _ in outs],
        scratch_shapes=[pltpu.VMEM(shape, jnp.float32) for shape in scratch],
        compiler_params=pltpu.CompilerParams(
            dimension_semantics=("arbitrary",), vmem_limit_bytes=VMEM_ASK
        ),
        cost_estimate=SMALL,
    )(*args)


def handed_on(source_ref, target_ref):
    target_ref[...] = source_ref[...]


def held_until(values, after):
    whole = shared(values.shape)
    return run_tiles(handed_on, 1, [(values, whole)], [(values.shape, values.dtype, whole)], (), after)[0]


def join_halves(place_ref, *refs):
    pairs = len(refs) // 3
    first = place_ref[0] == pl.program_id(0)
    for mine, other, out in zip(refs[:pairs], refs[pairs : 2 * pairs], refs[2 * pairs :]):

        @pl.when(first)
        def _(source=mine, target=out):
            target[...] = source[...]

        @pl.when(jnp.logical_not(first))
        def _(source=other, target=out):
            target[...] = source[...]


def joined_all(mine, other, place):
    ins = [(place.reshape((1,)), pl.BlockSpec(memory_space=pltpu.SMEM))]
    ins = ins + [(part, shared(part.shape)) for part in mine + other]
    outs = [
        ((2 * part.shape[0],) + part.shape[1:], part.dtype, banded(*part.shape)) for part in mine
    ]
    return run_tiles(join_halves, 2, ins, outs)


def cut_rows(source_ref, target_ref):
    rows = source_ref.shape[0] // target_ref.shape[0]
    pad = target_ref.shape[1] - rows
    values = source_ref[...].astype(jnp.float32)
    for k in range(target_ref.shape[0]):
        part = values[k * rows : (k + 1) * rows]
        if pad:
            part = jnp.concatenate([part, jnp.zeros((pad,) + part.shape[1:], jnp.float32)], axis=0)
        target_ref[k] = part.astype(target_ref.dtype)


def chunked(values, count):
    rows = values.shape[0] // count
    shape = (count, rows + -rows % 8) + values.shape[1:]
    return run_tiles(
        cut_rows, 1, [(values, shared(values.shape))], [(shape, values.dtype, shared(shape))]
    )[0]


class Mixer:

    def __init__(self, tokens, width, age, inner, tail, z, conv_w, conv_b, select_w, step_w, step_b, rates, skip, gain):
        self.tokens, self.width, self.tiles = tokens, width, width // LANE
        self.long = column(tokens)
        self.tall = banded(LANE, tokens)
        self.row = column(1)
        picked = shared((tokens, SELECTED))
        self.picked_spec = picked
        self.age = (age, shared((tokens, LANE)))
        self.conv = [
            (inner, self.tall), (tail, column(SUB)), self.age, (conv_w, column(CONV)), (conv_b, self.row),
            (select_w, column(SELECTED)),
        ]
        self.z = (z, self.tall)
        self.step_w = (step_w, column(SELECTED))
        self.step_b = (step_b, self.row)
        self.rates = (rates, column(STATE))
        self.skip, self.gain = (skip, self.row), (gain, self.row)
        self.wide = (tokens // SUB * STATE, SUB, LANE)
        self.states = (STATE, SUB, LANE)
        self.buffer = (tokens + SUB, LANE)

    def f32(self, rows, spec=None):
        return ((rows, self.width), jnp.float32, spec or column(rows))

    def low_out(self):
        return ((self.width, self.tokens), jnp.bfloat16, self.tall)

    def row_out(self):
        return ((SUB, self.tokens), jnp.float32, shared((SUB, self.tokens)))

    def picked_out(self):
        return ((self.tokens, SELECTED), jnp.float32, self.picked_spec)

    def states_out(self):
        return ((self.tiles,) + self.states, jnp.float32, tile_of(self.states))

    def run(self, body, ins, outs, scratch=(), after=()):
        return run_tiles(body, self.tiles, ins, outs, scratch, after)

    def first(self):
        mixed, picked = self.run(first_mixer, self.conv, [self.f32(self.tokens), self.picked_out()], [self.buffer])
        self.mixed = (mixed, self.long)
        return mixed, picked

    def totals(self, picked, after):
        self.picked = (picked, self.picked_spec)
        step, pre, end, part, span = self.run(
            scan_totals,
            [self.picked, self.mixed, self.age, self.step_w, self.step_b, self.rates],
            [self.f32(self.tokens)] * 2 + [self.f32(STATE + SUB), self.states_out(), self.f32(SUB)],
            [(self.tokens, GATES), self.wide],
            after,
        )
        self.step, self.pre = (step, self.long), (pre, self.long)
        self.part, self.span = (part, tile_of(self.states)), (span, column(SUB))
        return end

    def outputs(self, state_in, after):
        kept_shape = (self.wide[0] + STATE, SUB, LANE)
        mixed_out, value, squares, kept = self.run(
            scan_outputs,
            [self.step, self.mixed, self.age, self.picked, self.rates, self.part, self.span,
             (state_in, column(STATE)), self.skip, self.z],
            [self.f32(self.tokens)] * 2 + [self.row_out(),
             ((self.tiles,) + kept_shape, jnp.float32, tile_of(kept_shape))],
            [(self.tokens, GATES), self.wide, self.wide, (self.tokens, LANE)],
            after,
        )
        self.mixed_out, self.value = (mixed_out, self.long), (value, self.long)
        self.kept = (kept, tile_of(kept_shape))
        return squares[0]

    def normed(self, factor, gain):
        factor = jnp.broadcast_to(factor[None, :], (SUB, self.tokens))
        return self.run(
            normed,
            [self.value, (factor, shared((SUB, self.tokens))), (gain[:, None], banded(LANE, 1))],
            [self.low_out()],
        )[0]

    def norm_pull(self, grad):
        self.grad = (grad, self.tall)
        return self.run(
            norm_pull, [self.value, self.grad, self.gain], [self.row_out()], [(self.tokens, LANE)]
        )[0][0]

    def back_totals(self, factor, pull, after):
        stats = jnp.concatenate(
            [factor[None], pull[None], jnp.zeros((SUB - 2, self.tokens), jnp.float32)], axis=0
        )
        dmixed, dz, side, end, part = self.run(
            adjoint_totals,
            [self.value, self.grad, self.gain, (stats, shared((SUB, self.tokens))), self.z,
             self.mixed_out, self.mixed, self.step, self.age, self.picked, self.rates, self.span],
            [self.f32(self.tokens), self.low_out(), self.f32(SUB), self.f32(STATE), self.states_out()],
            [(self.tokens, GATES), self.wide, (self.tokens, LANE), (self.tokens, LANE)],
            after,
        )
        self.dmixed, self.back_part = (dmixed, self.long), (part, tile_of(self.states))
        return end, dz, side

    def back_grads(self, adjoint_in, after):
        direct, side, drates, dweight, dpicked = self.run(
            adjoint_grads,
            [self.step, self.mixed, self.age, self.dmixed, self.picked, self.rates, self.back_part, self.span,
             (adjoint_in, column(STATE)), self.kept, self.pre, self.step_w, self.skip],
            [self.f32(self.tokens), self.f32(SUB), self.f32(STATE), self.f32(SELECTED), self.picked_out()],
            [(self.tokens, GATES), self.wide, self.wide, self.states, self.wide, self.wide,
             (self.tokens, LANE), (self.tokens, LANE)],
            after,
        )
        self.direct = (direct, self.long)
        return side, drates, dweight, dpicked

    def last(self, dpicked, after):
        return self.run(
            last_mixer,
            self.conv + [(dpicked, self.picked_spec), self.direct, self.mixed],
            [self.low_out(), self.f32(2 * SUB), self.f32(SUB), self.f32(SELECTED)],
            [self.buffer, self.buffer],
            after,
        )


def over_rows(left_op, right_op):
    return lax.dot_general(
        left_op, right_op, (((0,), (0,)), ((), ())), preferred_element_type=jnp.float32
    )


def over_lanes(left_op, right_op):
    return lax.dot_general(
        left_op, right_op, (((1,), (1,)), ((), ())), preferred_element_type=jnp.float32
    )


def attend(repeats, query_ref, key_ref, value_ref, mask_ref, out_ref, total_ref):
    keys, values = key_ref[...], value_ref[...]
    for h in range(repeats):
        rows = slice(h * HD, (h + 1) * HD)
        scores = over_rows(keys, query_ref[rows, :]) + mask_ref[...]
        highest = jnp.max(scores, axis=0, keepdims=True)
        weights = jnp.exp(scores - highest)
        total = jnp.sum(weights, axis=0, keepdims=True)
        mixed = jnp.dot(values, weights.astype(jnp.bfloat16), preferred_element_type=jnp.float32)
        out_ref[rows, :] = mixed / total
        total_ref[0, h : h + 1, :] = highest + jnp.log(total)


def attend_back(
    repeats, query_ref, key_ref, value_ref, mask_ref, dout_ref, total_ref, delta_ref, place_ref,
    dquery_ref, dkey_ref, dvalue_ref,
):
    keys, values = key_ref[...], value_ref[...]
    reach = keys.shape[1] - META
    moved_to = pl.ds(pl.multiple_of(META + place_ref[0], LANE), reach)
    dkey_sum, dvalue_sum = 0.0, 0.0
    for h in range(repeats):
        rows = slice(h * HD, (h + 1) * HD)
        query, dout = query_ref[rows, :], dout_ref[rows, :]
        scores = over_rows(keys, query) + mask_ref[...]
        probs = jnp.exp(scores - total_ref[0, h : h + 1, :])
        dprobs = over_rows(values, dout)
        dscores = (probs * (dprobs - delta_ref[0, h : h + 1, :])).astype(jnp.bfloat16)
        probs = probs.astype(jnp.bfloat16)
        dquery_ref[rows, :] = jnp.dot(keys, dscores, preferred_element_type=jnp.float32)
        dkey_sum = dkey_sum + over_lanes(query, dscores)
        dvalue_sum = dvalue_sum + over_lanes(dout, probs)
    for target, found in ((dkey_ref, dkey_sum), (dvalue_ref, dvalue_sum)):
        target[...] = jnp.zeros_like(target)
        target[:, 0:META] = found[:, 0:META]
        target[:, moved_to] = found[:, META:]


def run_attention(query, keys, values, mask, after):
    count, reach = query.shape[1], keys.shape[1]
    tall = banded(HD * (H // KVH), count)
    stats = tile_of((SUB, count))
    keyed = banded(HD, reach)
    return run_tiles(
        functools.partial(attend, H // KVH),
        KVH,
        [(query, tall), (keys, keyed), (values, keyed), (mask, shared((reach, count)))],
        [(query.shape, jnp.float32, tall), ((KVH, SUB, count), jnp.float32, stats)],
        (),
        after,
    )


def run_attention_back(query, keys, values, mask, dout, totals, delta, place, spread, after):
    count, reach = query.shape[1], keys.shape[1]
    tall = banded(HD * (H // KVH), count)
    stats = tile_of((SUB, count))
    keyed = banded(HD, reach)
    found = ((keys.shape[0], spread), jnp.float32, banded(HD, spread))
    return run_tiles(
        functools.partial(attend_back, H // KVH),
        KVH,
        [
            (query, tall), (keys, keyed), (values, keyed), (mask, shared((reach, count))), (dout, tall),
            (totals, stats), (delta, stats), (place, pl.BlockSpec(memory_space=pltpu.SMEM)),
        ],
        [(query.shape, jnp.float32, tall), found, found],
        (),
        after,
    )


def dot_plain(left_op, right_op):
    return jnp.dot(left_op, right_op, preferred_element_type=jnp.float32)


def dot_left(left_op, right_op):
    return lax.dot_general(
        left_op, right_op, (((0,), (0,)), ((), ())), preferred_element_type=jnp.float32
    )


def dot_right(left_op, right_op):
    return lax.dot_general(
        left_op, right_op, (((1,), (1,)), ((), ())), preferred_element_type=jnp.float32
    )


def exact_dot(left_op, right_op):
    return jnp.dot(left_op, right_op, precision=HIGH, preferred_element_type=jnp.float32)


def exact_left(left_op, right_op):
    return lax.dot_general(
        left_op,
        right_op,
        (((0,), (0,)), ((), ())),
        precision=HIGH,
        preferred_element_type=jnp.float32,
    )


def exact_right(left_op, right_op):
    return lax.dot_general(
        left_op,
        right_op,
        (((1,), (1,)), ((), ())),
        precision=HIGH,
        preferred_element_type=jnp.float32,
    )


def low(values):
    return values.astype(jnp.bfloat16)


def wide(values):
    return values.astype(jnp.float32)


def swapped(values, axis):
    return straight(lax.ppermute(straight(values), axis, [(0, 1), (1, 0)]))


def moved(values, axis, distance):
    count = lax.axis_size(axis)
    route = [(i, i + distance) for i in range(count) if 0 <= i + distance < count]
    return lax.ppermute(values, axis, route)


def joined(mine, other, place):
    which = lax.broadcasted_iota(jnp.int32, (2,) + (1,) * mine.ndim, 0)
    both = jnp.where(which == place, mine[None], other[None])
    return both.reshape((2 * mine.shape[0],) + mine.shape[1:])


def chosen(pieces, place):
    result = pieces[0]
    for index, piece in enumerate(pieces[1:], 1):
        result = jnp.where(place == index, piece, result)
    return result


def pieces_of(values, count, axis):
    size = values.shape[axis] // count
    return [lax.slice_in_dim(values, i * size, (i + 1) * size, axis=axis) for i in range(count)]


def group_total(values):
    over_cols = values + swapped(values, "col")
    return over_cols + swapped(over_cols, "row")


def straight(values):
    return with_layout_constraint(values, Layout(tuple(range(values.ndim))))


def kept_apart(values, place, size, axis=0):
    mine = lax.dynamic_slice_in_dim(values, place * size, size, axis=axis)
    away = lax.dynamic_slice_in_dim(values, (1 - place) * size, size, axis=axis)
    return mine, away


class SeqSum:

    def __init__(self, left, right, scale=1.0, flip=False, after=(), rows=None):
        self.count, self.place = lax.axis_size("seq"), lax.axis_index("seq")
        self.bits = self.count.bit_length() - 1
        self.right, self.scale, self.flip = right, scale, flip
        if left.ndim == 2:
            left = left.reshape((self.count, left.shape[0] // self.count) + left.shape[1:])
        self.rows = rows or left.shape[1]
        self.left = left.reshape((2,) * self.bits + left.shape[1:])
        self.stage = 0
        self.send(low(self.product(self.half(self.left, True, after))))

    def half(self, values, away, after=()):
        bit = (self.place // 2**self.stage) % 2
        which = (1 - bit if away else bit) + nothing(*after)
        return lax.dynamic_index_in_dim(
            values, which, self.bits - 1 - self.stage, keepdims=False
        )

    def product(self, left):
        operands = (self.right, left) if self.flip else (left, self.right)
        dims = ((operands[0].ndim - 1,), (operands[1].ndim - 1,))
        found = lax.dot_general(
            *operands, (dims, ((), ())), preferred_element_type=jnp.float32
        )
        return self.scale * (jnp.moveaxis(found, 0, -2) if self.flip else found)

    def send(self, values):
        self.sent = straight(values)
        route = [(i, i ^ 2**self.stage) for i in range(self.count)]
        self.got = straight(lax.ppermute(self.sent, "seq", route))

    def step(self, *after):
        if self.stage == 0:
            mine = self.product(self.half(self.left, False, after))
        else:
            mine = wide(self.half(self.now, False, after))
        total = mine + wide(self.got)
        self.stage += 1
        if self.stage == self.bits:
            self.total = total
        else:
            self.now = straight(low(total))
            self.send(self.half(self.now, True))
        return self

    def finish(self, *after):
        while self.stage < self.bits:
            self.step(*after)
        rows = self.rows
        return self.total[:, :rows] if self.flip else self.total[:rows]


def seq_reduce(values):
    count, place = lax.axis_size("seq"), lax.axis_index("seq")
    bits = count.bit_length() - 1
    parts = values.reshape((2,) * bits + (values.shape[0] // count,) + values.shape[1:])
    for stage in range(bits):
        bit = (place // 2**stage) % 2
        axis = bits - 1 - stage
        mine = lax.dynamic_index_in_dim(parts, bit, axis, keepdims=False)
        away = lax.dynamic_index_in_dim(parts, 1 - bit, axis, keepdims=False)
        route = [(i, i ^ 2**stage) for i in range(count)]
        parts = mine + wide(lax.ppermute(low(away), "seq", route))
    return parts


def told(values, axes):
    count = lax.axis_size(axes)
    return lax.all_to_all(
        jnp.broadcast_to(values[None], (count,) + values.shape), axes, split_axis=0, concat_axis=0
    )


def all_total(values):
    count = lax.axis_size(ALL)
    shares = lax.all_to_all(values.reshape(count, -1), ALL, split_axis=0, concat_axis=0, tiled=True)
    return told(jnp.sum(shares, axis=0), ALL).reshape(-1)


def turned(values, cosine, sine, back):
    heads = values.reshape((values.shape[0] // HD, 2, HD // 2) + values.shape[1:])
    first, second = heads[:, :1], heads[:, 1:]
    sine = -sine if back else sine
    turned_pair = [first * cosine - second * sine, second * cosine + first * sine]
    return jnp.concatenate(turned_pair, axis=1).reshape(values.shape)


def entering_state(ends, spans, rates, reverse):
    count, place = lax.axis_size("seq"), lax.axis_index("seq")
    state = jnp.zeros_like(ends[0])
    for k in range(count):
        at = count - 1 - k if reverse else k
        reached = at > place if reverse else at < place
        decay = jnp.exp2(rates * spans[at][None, :])
        state = jnp.where(reached, decay * state + ends[at], state)
    return state


def shards(
    hidden_in,
    grad_out,
    segment_ids,
    pre_gain,
    qkv_weight,
    mixer_in_weight,
    meta_cache,
    conv_weight,
    conv_bias,
    select_weight,
    step_weight,
    step_bias,
    log_rates,
    skip_gain,
    attn_gain,
    mixer_gain,
    attn_out_weight,
    mixer_out_weight,
    post_gain,
    gate_weight,
    up_weight,
    down_weight,
):
    row, col, seq = lax.axis_index("row"), lax.axis_index("col"), lax.axis_index("seq")
    tokens = hidden_in.shape[0]
    quarter = DI // 4
    half = D // 2
    lanes = -(-quarter // LANE) * LANE
    member = 2 * row + col

    def by_row(first, second):
        return jnp.where(row == 0, first, second)

    def row_joined(values):
        return joined(values, swapped(values, "row"), row)

    def col_joined(values):
        return joined(values, swapped(values, "col"), col)

    def col_summed(part):
        mine, away = kept_apart(part, col, part.shape[0] // 2)
        return mine + wide(swapped(low(away), "col"))

    def row_summed(part):
        part = low(part)
        return wide(part) + wide(swapped(part, "row"))

    def row_scattered(part):
        mine, away = kept_apart(part, row, part.shape[0] // 2)
        return mine + wide(swapped(low(away), "row"))

    def over_cols(values):
        return values + swapped(values, "col")

    hidden_m = row_joined(hidden_in.T)
    gains_m = row_joined(jnp.stack([pre_gain, post_gain], axis=1))
    pre_g, post_g = gains_m[:, :1], gains_m[:, 1:]
    hm = wide(hidden_m)
    pre_factor = lax.rsqrt(over_cols(jnp.sum(hm * hm, axis=0)) / D + EPS)[None, :]
    first_m = low(hm * pre_factor * pre_g)

    inner_part = straight(over_rows(mixer_in_weight, first_m))
    near, far = inner_part[: 2 * quarter], inner_part[2 * quarter :]
    near_m, near_away = kept_apart(near, col, quarter)
    far_m, far_away = kept_apart(far, col, quarter)
    give_m, keep_m = by_row(far_m, near_m), by_row(near_m, far_m)
    give_got = swapped(low(by_row(far_away, near_away)), "col")
    keep_got = swapped(low(by_row(near_away, far_away)), "col")
    given = low(give_m + wide(give_got))
    taken = swapped(given, "row")
    kept_in = low(keep_m + wide(keep_got))
    qkv_part = low(col_summed(over_rows(qkv_weight, first_m)))
    qkv_core = lax.all_to_all(qkv_part, GROUP, split_axis=1, concat_axis=0, tiled=True)
    def filled(values):
        return jnp.pad(values, ((0, lanes - quarter), (0, 0)))

    def channels(values, axis):
        part = chosen(pieces_of(values, 4, axis), member)
        sides = [(0, lanes - quarter) if i == axis else (0, 0) for i in range(values.ndim)]
        return jnp.pad(part, sides)

    inner_own = filled(by_row(kept_in, taken))
    gate_z = filled(by_row(taken, kept_in))

    own_tokens = tokens // 4
    devices_back = (WIN + own_tokens - 2) // own_tokens
    halo_rows = devices_back * own_tokens
    tail_rows = CONV - 1
    kv_width = KVH * HD
    start_row = seq * tokens + member * own_tokens
    seg_padded = jnp.concatenate([jnp.full((halo_rows,), -1, jnp.int32), segment_ids])
    key_segs = lax.dynamic_slice(seg_padded, (start_row,), (halo_rows + own_tokens,))
    query_segs = key_segs[halo_rows:]
    query_glob = start_row + jnp.arange(own_tokens, dtype=jnp.int32)
    key_glob = start_row - halo_rows + jnp.arange(halo_rows + own_tokens, dtype=jnp.int32)
    doc_start = jnp.sum((segment_ids[:, None] < query_segs[None, :]).astype(jnp.int32), axis=0)
    frequency = THETA ** (-2.0 * jnp.arange(HD // 2, dtype=jnp.float32) / HD)
    angles = frequency[:, None] * wide(query_glob - doc_start)[None, :]
    cosine, sine = jnp.cos(angles), jnp.sin(angles)
    score_scale = HD ** (-0.5)
    query = low(turned(wide(qkv_core[:D]), cosine, sine, False) * score_scale)
    key_own = low(turned(wide(qkv_core[D : D + kv_width]), cosine, sine, False))
    pair_own = jnp.concatenate([key_own, qkv_core[D + kv_width :]], axis=0)
    groups_back = (WIN + tokens - 2) // tokens
    distance = query_glob[None, :] - key_glob[:, None]
    visible = (key_segs[:, None] == query_segs[None, :]) & (distance >= 0) & (distance < WIN)
    mask = jnp.where(
        jnp.concatenate([jnp.ones((META, own_tokens), jnp.bool_), visible], axis=0), 0.0, NEG
    )

    conv_w, conv_b = channels(conv_weight, 1), channels(conv_bias, 0)
    select_w, step_w = channels(select_weight.T, 1), channels(step_weight, 1)
    step_b, skip_g = channels(step_bias, 0), channels(skip_gain, 0)
    mixer_g = channels(mixer_gain, 0)
    decay_rates = jnp.exp(channels(log_rates, 0).T)
    valid = lax.broadcasted_iota(jnp.int32, (1, lanes), 1) < quarter
    rates = jnp.where(valid, -LOG2E * decay_rates, 0.0)

    edge = wide(inner_own[:, tokens - LANE :])[:, LANE - tail_rows :].T
    tail = jnp.pad(moved(edge, "seq", 1), ((SUB - tail_rows, 0), (0, 0)))
    conv_segs = lax.dynamic_slice(
        seg_padded, (seq * tokens + halo_rows - tail_rows,), (tokens + tail_rows,)
    )
    own_segs = conv_segs[tail_rows:]
    age = sum(wide(conv_segs[tap : tap + tokens] == own_segs) for tap in range(tail_rows))
    age = jnp.broadcast_to(age[:, None], (tokens, LANE))
    step_w = jnp.pad(step_w, ((0, SELECTED - DT_RANK), (0, 0)))
    mixer = Mixer(
        tokens, lanes, age, inner_own, tail, gate_z, conv_w, conv_b[None], select_w, step_w, step_b[None],
        rates, skip_g[None], mixer_g[None],
    )
    mixed_in, picked = mixer.first()
    picked = picked + swapped(picked, "col")
    pairs = told(pair_own, GROUP)
    pair_group = jnp.concatenate(
        [
            lax.dynamic_index_in_dim(pairs, i + nothing(picked), 0, keepdims=False)
            for i in range(pairs.shape[0])
        ],
        axis=1,
    )
    halo = [moved(pair_group, "seq", offset) for offset in range(groups_back, 0, -1)]
    skipped = (groups_back * tokens - halo_rows) + member * own_tokens
    window = lax.dynamic_slice_in_dim(
        jnp.concatenate(halo + [pair_group], axis=1), skipped, halo_rows + own_tokens, axis=1
    )
    meta_pair = meta_cache.transpose(0, 2, 1).reshape(2 * kv_width, META)
    pair_all = jnp.concatenate([meta_pair, window], axis=1)
    selected = picked + swapped(picked, "row")
    end = mixer.totals(selected, ())
    attn, log_totals = run_attention(query, pair_all[:kv_width], pair_all[kv_width:], mask, (end,))
    ends = told(end, "seq")
    spans = ends[:, STATE, :]
    state_in = entering_state(ends[:, :STATE], spans, rates, False)

    attn_factor = lax.rsqrt(jnp.mean(attn * attn, axis=0, keepdims=True) + EPS)
    attn_low = low(attn * attn_factor * attn_gain[:, None] + wide(nothing(ends)))
    attn_part = lax.all_to_all(attn_low, GROUP, split_axis=0, concat_axis=1, tiled=True)
    attn_rows = col_joined(attn_part)
    grad_m = row_joined(grad_out.T)
    seq_count = lax.axis_size("seq")
    grad_chunks = chunked(grad_m, seq_count)
    down_t, mixer_out_t = down_weight.T, mixer_out_weight.T
    dact = col_summed(over_rows(down_t, held_until(grad_m, [end])))

    squares = mixer.outputs(state_in, (attn_rows, dact, grad_chunks))
    mixer_factor = lax.rsqrt(group_total(squares) / DI + EPS)
    mixer_rows = col_joined(mixer.normed(mixer_factor, mixer_g)[:quarter])

    mix_m = row_summed(
        0.5 * (over_rows(attn_out_weight, attn_rows) + dot_plain(mixer_out_t, mixer_rows))
    )
    resid_m = hm + mix_m
    post_factor = lax.rsqrt(over_cols(jnp.sum(resid_m * resid_m, axis=0)) / D + EPS)[None, :]
    second_m = low(resid_m * post_factor * post_g)
    gate_act = col_summed(over_rows(gate_weight, second_m))
    up_act = col_summed(over_rows(up_weight, second_m))
    sig_gate = jax.nn.sigmoid(gate_act)
    dgate_low = low(dact * up_act * sig_gate * (1.0 + gate_act * (1.0 - sig_gate)))
    dup_low = low(dact * gate_act * sig_gate)
    act_low = low(gate_act * sig_gate * up_act)
    ffn_low = [dgate_low, dup_low, act_low]
    ffn_other = [swapped(part, "col") for part in ffn_low]
    dgate_rows, dup_rows, act_rows = joined_all(ffn_low, ffn_other, col)
    dsecond_m = row_summed(dot_plain(gate_weight, dgate_rows) + dot_plain(up_weight, dup_rows))
    sum_gate = SeqSum(dgate_rows, second_m, 1.0, True)
    sum_up = SeqSum(dup_rows, second_m, 1.0, True)
    weighted_m = dsecond_m * post_g
    inner_sum = over_cols(jnp.sum(weighted_m * resid_m, axis=0)) / D
    pull_back = post_factor**3 * inner_sum[None, :]
    dmid_m = wide(grad_m) + post_factor * weighted_m - resid_m * pull_back
    post_part = jnp.sum(dsecond_m * resid_m * post_factor, axis=1)
    low_m = low(dmid_m)

    dmixer_low = filled(low(0.5 * col_summed(over_rows(mixer_out_t, low_m))))
    dattn_part = low(0.5 * col_summed(dot_plain(attn_out_weight, low_m)))
    dattn_core = lax.all_to_all(dattn_part, GROUP, split_axis=1, concat_axis=0, tiled=True)

    mixer_sum = group_total(mixer.norm_pull(dmixer_low)) / DI
    back_end, dz_own, side_norm = mixer.back_totals(
        mixer_factor,
        mixer_factor**3 * mixer_sum,
        [sum_gate.sent, sum_up.sent],
    )
    adjoint_in = entering_state(told(back_end, "seq"), spans, rates, True)

    incoming = wide(dattn_core)
    attn_weighted = incoming * attn_gain[:, None]
    attn_sum = jnp.mean(attn_weighted * attn, axis=0, keepdims=True)
    dattn = low(attn_factor * attn_weighted - attn * (attn_factor**3 * attn_sum))
    attn_gain_part = jnp.sum(incoming * attn * attn_factor, axis=1)
    delta = jnp.sum((wide(dattn) * attn).reshape(H, HD, own_tokens), axis=1)
    delta = jnp.pad(
        delta.reshape(KVH, H // KVH, own_tokens), ((0, 0), (0, SUB - H // KVH), (0, 0))
    )
    reach = groups_back * tokens
    dquery, dkey, dvalue = run_attention_back(
        query, pair_all[:kv_width], pair_all[kv_width:], mask, dattn, log_totals, delta,
        skipped.reshape((1,)), META + reach + tokens,
        [back_end, sum_gate.got],
    )
    sum_gate.step(dquery)
    sum_up.step(sum_gate.now)

    sum_down = SeqSum(grad_chunks, act_rows, 1.0, False, [adjoint_in], grad_m.shape[0] // seq_count)
    both_rows = jnp.concatenate([attn_rows, mixer_rows], axis=0)
    sum_out = SeqSum(chunked(low_m, seq_count), both_rows, 0.5, False, [adjoint_in], low_m.shape[0] // seq_count)
    side_step, drates, step_weight_part, dpicked = mixer.back_grads(
        adjoint_in,
        [sum_gate.now, sum_up.now, sum_down.sent, sum_out.sent],
    )
    dpicked = held_until(dpicked, [sum_gate.got, sum_up.got, sum_down.got, sum_out.got])
    sums = [sum_gate, sum_up, sum_out, sum_down]
    for part in sums:
        part.step(drates)
    dinner_own, edges, side_conv, select_part = mixer.last(
        group_total(dpicked),
        [],
    )
    held = wide(nothing(drates))
    dgroup = jnp.concatenate([dkey[:, META + reach :], dvalue[:, META + reach :]], axis=0)
    dgroup = dgroup + wide(nothing(select_part))
    for offset in range(1, groups_back + 1):
        at = slice(META + reach - offset * tokens, META + reach - (offset - 1) * tokens)
        piece = low(jnp.concatenate([dkey[:, at], dvalue[:, at]], axis=0) + held)
        dgroup = dgroup + wide(moved(piece, "seq", -offset))
    shares = lax.all_to_all(
        low(dgroup).reshape(2 * kv_width, 4, own_tokens), GROUP, split_axis=1, concat_axis=1
    )
    dpair_own = jnp.sum(wide(shares), axis=1)
    dquery = turned(dquery * score_scale, cosine, sine, True)
    dkey_own = turned(dpair_own[:kv_width], cosine, sine, True)
    dqkv_core = low(
        jnp.concatenate([dquery, dkey_own, dpair_own[kv_width:]], axis=0)
    )
    dqkv_part = lax.all_to_all(dqkv_core, GROUP, split_axis=0, concat_axis=1, tiled=True)
    dqkv_rows = col_joined(dqkv_part)
    sum_qkv = SeqSum(chunked(dqkv_rows, seq_count), first_m, 1.0, False, (), dqkv_rows.shape[0] // seq_count)

    lost = moved(edges[SUB - tail_rows : SUB], "seq", -1)
    ending = low(edges[2 * SUB - tail_rows :] + lost).T
    dinner_own = lax.dynamic_update_slice(
        dinner_own, ending, (nothing(*[part.got for part in sums]), tokens - tail_rows)
    )[:quarter]
    dz_t = dz_own[:quarter]
    got_back = swapped(by_row(dz_t, dinner_own), "row")
    dnear = col_joined(by_row(dinner_own, got_back))
    dfar = col_joined(by_row(got_back, dz_t))
    dinner_rows = jnp.concatenate([dnear, dfar], axis=0)
    dchunks = dinner_rows.reshape(lax.axis_size("seq"), -1, tokens)
    cut = dchunks.shape[1] // 16 * 8
    params = jnp.concatenate(
        [
            select_part,
            step_weight_part[:DT_RANK],
            drates,
            side_conv[: CONV + 1],
            side_step[:1],
            side_norm[:2],
        ],
        axis=0,
    )
    count = lax.axis_size("seq")
    shares = low(params).reshape((count, -1) + params.shape[1:])
    shares = lax.all_to_all(shares, "seq", split_axis=0, concat_axis=0, tiled=True)
    params = jnp.sum(wide(shares), axis=0)
    spread_out = told(low(params), "seq")
    spread_out = joined(spread_out, swapped(spread_out, "row"), row)
    spread_out = joined(spread_out, swapped(spread_out, "col"), col)
    spread_out = spread_out.reshape((2, 2, -1, lanes))
    params = jnp.concatenate(
        [wide(spread_out[q % 2, q // 2][:, :quarter]) for q in range(4)], axis=1
    )

    def block(values):
        return lax.dynamic_slice_in_dim(values, row * (half // 2), half // 2, axis=0)

    gain_block = pre_gain.shape[0]
    block_pos = (2 * col + row) * gain_block

    def spread(part):
        return lax.dynamic_update_slice(jnp.zeros((D,), jnp.float32), part, (block_pos,))

    sums_in = [
        SeqSum(dchunks[:, :cut].reshape(-1, tokens), first_m, 1.0, False, [spread_out]),
        SeqSum(dchunks[:, cut:].reshape(-1, tokens), first_m),
    ]
    begun = [part.sent for part in sums_in]
    sum_out.step(*begun)
    sum_down.step(*begun)

    dfirst_part = dot_plain(qkv_weight, dqkv_rows) + dot_plain(mixer_in_weight, dinner_rows)
    dfirst_part = dfirst_part + wide(nothing(*begun))
    first_sum = group_total(jnp.sum(dfirst_part * pre_g * hm, axis=0)) / D

    dfirst = row_scattered(dfirst_part)
    own_hidden = block(hm)
    grad_in = (
        block(dmid_m)
        + pre_factor * dfirst * block(pre_g)
        - own_hidden * (pre_factor**3 * first_sum[None, :])
    )
    pre_part = jnp.sum(dfirst * own_hidden * pre_factor, axis=1)
    out_part = dot_plain(down_t, act_rows) + wide(nothing(*begun))
    hidden_out = low(block(resid_m) + row_scattered(out_part))


    pre_parts = told(pre_part, ALL).reshape((count, 2, 2, gain_block))
    pre_grad = jnp.sum(pre_parts, axis=0).transpose(1, 0, 2).reshape(-1)
    out_grads = sum_out.finish(*begun)
    sums_in[0].step(*begun)
    sums_in[1].step(sums_in[0].now)
    early = all_total(
        jnp.concatenate(
            [
                (dkey[:, :META] + wide(nothing(sums_in[1].now))).reshape(-1),
                dvalue[:, :META].reshape(-1),
                attn_gain_part,
                spread(block(post_part[:, None])[:, 0]),
            ]
        )
    )
    meta_size = 2 * kv_width * META
    meta_grad = early[:meta_size].reshape(2, kv_width, META).transpose(0, 2, 1)
    attn_gain_grad = early[meta_size : meta_size + D]
    post_grad = early[meta_size + D :]
    sums_in[0].step(sums_in[1].now)
    sums_in[1].step(sums_in[0].now)
    sum_qkv.step(sums_in[1].now)
    ranks = DT_RANK + 2 * STATE
    at_rates = ranks + DT_RANK
    at_conv = at_rates + STATE
    return (
        hidden_out.T,
        grad_in.T,
        pre_grad,
        sum_qkv.finish(*begun).T,
        jnp.concatenate([piece.finish(params) for piece in sums_in], axis=0).T,
        meta_grad,
        params[at_conv : at_conv + CONV],
        params[at_conv + CONV],
        params[:ranks].T,
        params[ranks:at_rates],
        params[at_conv + CONV + 1],
        params[at_rates:at_conv].T,
        params[at_conv + CONV + 2],
        attn_gain_grad,
        params[at_conv + CONV + 3],
        out_grads[:, :half].T,
        out_grads[:, half:].T,
        post_grad,
        sum_gate.finish(*begun),
        sum_up.finish(*begun),
        sum_down.finish(*begun).T,
    )


def solution(mesh):
    in_specs = (
        P("seq", ("col", "row")),
        P("seq", ("col", "row")),
        P(),
        P(("col", "row")),
        P("col", "row"),
        P("col", "row"),
        P(),
        P(),
        P(),
        P(),
        P(),
        P(),
        P(),
        P(),
        P(),
        P(),
        P("row", "col"),
        P("row", "col"),
        P(("col", "row")),
        P("col", "row"),
        P("col", "row"),
        P("row", "col"),
    )
    out_specs = (
        P("seq", ("col", "row")),
        P("seq", ("col", "row")),
        P(),
        P("col", ("row", "seq")),
        P("col", ("row", "seq")),
        P(),
        P(),
        P(),
        P(),
        P(),
        P(),
        P(),
        P(),
        P(),
        P(),
        P("row", ("col", "seq")),
        P("row", ("col", "seq")),
        P(),
        P("col", ("row", "seq")),
        P("col", ("row", "seq")),
        P("row", ("col", "seq")),
    )
    return jax.shard_map(shards, mesh=mesh, in_specs=in_specs, out_specs=out_specs, check_vma=False)
```
